32 devices in a mesh: slab: 4 (over x, core), seq: 8 (over z, y).
Axes of the slice: x: 2, y: 2, z: 4, core: 2. Of those that a mesh axis runs over, the one named last changes fastest.
Arguments:
- stream: bfloat16 [4, 384, 1536], P('slab', 'seq'), may hold values from -40 to 40
- latents: float32 [4, 384, 64], P('slab', 'seq'), may hold values from -6 to 6
- time_mod: float32 [4, 3, 1536], P('slab'), may hold values from -4 to 4
- block_mod: float32 [3, 1536], replicated, may hold values from -4 to 4
- w_qkv: bfloat16 [1536, 3072], P(None, 'seq'), may hold values from -0.15625 to 0.15625
- qk_gain: float32 [2, 1024], replicated, may hold values from 0.5 to 9
- w_out: bfloat16 [1024, 1536], replicated, may hold values from -0.1875 to 0.1875
- head_mod: float32 [4, 2, 1536], P('slab'), may hold values from -4 to 4
- w_head: bfloat16 [1536, 64], replicated, may hold values from -0.15625 to 0.15625
- noise_level: int32 [4], P('slab'), may hold values from 1 to 32, as said below
Outputs:
- new_stream: bfloat16 [4, 384, 1536], P('slab', 'seq')
- next_latents: float32 [4, 384, 64], P('slab', 'seq')
The draws below stay inside these ranges and needn't reach their ends.
Inputs may be any that keep to these rules, and one draw needn't show every extreme that they name: noise_level rises strictly along the groups; the first group has level 1 and the last has level 32.
All inputs are finite; a program needn't handle non-finite values.
Results may differ from the reference program's by a relative error of at most 0.0056.
The reference program's roundings to bfloat16 on the way count: a program that leaves them out, or rounds other values in their place, can miss the bound.
Values may be sent and summed in bfloat16 or wider, within the bound.
No kernel may reach another device: no remote copies, remote signals or barrier semaphores. Data moves between devices by JAX's collectives and lax.ppermute only.
A program may use at most 128 MiB of HBM per device.

```python
import math
import jax
import jax.numpy as jnp
from jax import lax

D = 1536
HEADS = 8
HEAD_DIM = 128
CHAN = 64
LEVELS = 32
ATT = 1024
GROUP = 384
SLABS = 4


def draw_stream(key, part):
    key = jax.random.fold_in(key, 5)
    key_base, key_rows, key_cols, key_dir = jax.random.split(key, 4)
    base = jax.random.truncated_normal(key_base, -4.0, 4.0, (SLABS, GROUP, D), jnp.float32)
    row_scale = jnp.exp(jax.random.uniform(key_rows, (SLABS, GROUP, 1), jnp.float32, math.log(0.3), math.log(3.0)))
    col_scale = jnp.exp(jax.random.uniform(key_cols, (D,), jnp.float32, math.log(0.5), math.log(2.0)))
    direction = 0.7 * jax.random.truncated_normal(key_dir, -4.0, 4.0, (SLABS, 1, D), jnp.float32)
    return ((base * col_scale + direction) * row_scale).astype(jnp.bfloat16)


def draw_qk_gain(key, part):
    key = jax.random.fold_in(key, 7)
    key_level, key_jitter = jax.random.split(key, 2)
    lowest, largest = (0.7, 2.2)
    levels = jnp.exp(jax.random.uniform(key_level, (2, HEADS, 1), jnp.float32, math.log(lowest), math.log(largest)))
    jitter = jax.random.uniform(key_jitter, (2, HEADS, HEAD_DIM), jnp.float32, 0.85, 1.15)
    return (levels * jitter).reshape(2, HEADS * HEAD_DIM)


def draw_noise_level(key, part):
    key = jax.random.fold_in(key, 11)
    shuffled = jax.random.permutation(key, LEVELS - 2) + 2
    middle = jnp.sort(shuffled[:SLABS - 2]).astype(jnp.int32)
    return jnp.concatenate([jnp.array([1], jnp.int32), middle, jnp.array([LEVELS], jnp.int32)])


def block_scale(own_key, shape, cuts, least, high):
    level = 1.0
    for axis_at, shards_of in cuts:
        steps = jax.random.uniform(jax.random.fold_in(jax.random.fold_in(own_key, 6), axis_at), (shards_of,), jnp.float32, least / len(cuts), high / len(cuts))
        level = level * jnp.repeat(jnp.exp(steps), shape[axis_at] // shards_of).reshape((-1,) + (1,) * (len(shape) - 1 - axis_at))
    return level


def centred(rng, extent, deviation, most, cuts=(), dtype=jnp.bfloat16):
    factor_of = block_scale(rng, extent, cuts, -0.22, 0.18) if cuts else 1.0
    values = jax.random.normal(rng, extent, jnp.float32) * deviation * factor_of
    return jnp.minimum(jnp.maximum(values, -most), most).astype(dtype)


def setup_inputs(seed: int = 0) -> dict:
    splits = jax.random.split(jax.random.key(seed), 11)
    return {
        "stream": draw_stream(jax.random.fold_in(splits[10], 71), 0),
        "latents": centred(splits[1], (SLABS, GROUP, CHAN), 1.0, 6.0, ((0, 4), (1, 8)), jnp.float32),
        "time_mod": centred(splits[2], (SLABS, 3, D), 0.6, 4.0, ((0, 4),), jnp.float32),
        "block_mod": centred(splits[3], (3, D), 0.4, 4.0, (), jnp.float32),
        "w_qkv": centred(splits[4], (D, 3 * ATT), D ** -0.5, 0.15625, ((1, 8),)),
        "qk_gain": draw_qk_gain(jax.random.fold_in(splits[10], 71), 0),
        "w_out": centred(splits[6], (ATT, D), ATT ** -0.5, 0.1875),
        "head_mod": centred(splits[7], (SLABS, 2, D), 0.5, 4.0, ((0, 4),), jnp.float32),
        "w_head": centred(splits[8], (D, CHAN), D ** -0.5, 0.15625),
        "noise_level": draw_noise_level(jax.random.fold_in(splits[10], 71), 0),
    }


def layer_norm(values):
    center = values - lax.optimization_barrier(jnp.mean(values, axis=-1, keepdims=True))
    spread = lax.optimization_barrier(jnp.mean(center * center, axis=-1, keepdims=True))
    return center * lax.rsqrt(spread + 1e-06)

def sigma_table():
    fraction = jnp.arange(LEVELS + 1).astype(jnp.float32) / LEVELS
    return 5.0 * fraction / (1.0 + 4.0 * fraction)

def norm_rope(values, gain_row, position):
    row_count = values.shape[0]
    floats = values.astype(jnp.float32)
    scaled = floats * lax.rsqrt(lax.optimization_barrier(jnp.mean(floats * floats, axis=-1, keepdims=True)) + 1e-06) * gain_row
    halves = HEAD_DIM // 2
    scaled = scaled.reshape(row_count, HEADS, HEAD_DIM)
    frequency = jnp.power(10000.0, -jnp.arange(halves).astype(jnp.float32) / halves)
    angles = position[:, None, None] * frequency[None, None, :]
    cosines = jnp.cos(angles)
    sines = jnp.sin(angles)
    front_half = scaled[..., :halves]
    back_half = scaled[..., halves:]
    turned = jnp.concatenate([front_half * cosines - back_half * sines, front_half * sines + back_half * cosines], axis=-1)
    return turned.reshape(row_count, ATT).astype(jnp.bfloat16)

def group_parts(queries, key_rows, value_rows):
    row_count = queries.shape[0]
    key_count = key_rows.shape[0]
    query_heads = queries.astype(jnp.float32).reshape(row_count, HEADS, HEAD_DIM)
    key_heads = key_rows.astype(jnp.float32).reshape(key_count, HEADS, HEAD_DIM)
    value_heads = value_rows.astype(jnp.float32).reshape(key_count, HEADS, HEAD_DIM)
    scores = jnp.einsum('rhd,khd->hrk', query_heads, key_heads) * HEAD_DIM ** (-0.5)
    maxima = lax.optimization_barrier(jnp.max(scores, axis=-1))
    weights = jnp.exp(scores - maxima[..., None]).astype(jnp.bfloat16)
    totals = lax.optimization_barrier(jnp.sum(weights.astype(jnp.float32), axis=-1))
    output = jnp.einsum('hrk,khd->rhd', weights.astype(jnp.float32), value_heads)
    return (output, maxima.T, totals.T)

def reference(stream, latents, time_mod, block_mod, w_qkv, qk_gain, w_out, head_mod, w_head, noise_level):
    hidden = stream.astype(jnp.float32)
    modulation = block_mod[None] + time_mod
    modded = (layer_norm(hidden) * (1.0 + modulation[:, 1:2]) + modulation[:, 0:1]).astype(jnp.bfloat16)
    mixed = jnp.dot(modded.reshape(SLABS * GROUP, D), w_qkv, preferred_element_type=jnp.float32).astype(jnp.bfloat16)
    position = jnp.arange(SLABS * GROUP).astype(jnp.float32)
    queries = norm_rope(mixed[:, :ATT], qk_gain[0], position).reshape(SLABS, GROUP, ATT)
    key_rows = norm_rope(mixed[:, ATT:2 * ATT], qk_gain[1], position).reshape(SLABS, GROUP, ATT)
    value_rows = mixed[:, 2 * ATT:].reshape(SLABS, GROUP, ATT)
    highest = jnp.full((SLABS * GROUP, HEADS), -1e+30, jnp.float32)
    sums = jnp.zeros((SLABS * GROUP, HEADS), jnp.float32)
    accum = jnp.zeros((SLABS * GROUP, HEADS, HEAD_DIM), jnp.float32)
    for owner in range(SLABS):
        start_row = owner * GROUP
        output, maxima, totals = group_parts(queries[owner:].reshape(-1, ATT), key_rows[owner], value_rows[owner])
        old_high = highest[start_row:]
        new_high = jnp.maximum(old_high, maxima)
        keep_old = jnp.exp(old_high - new_high)
        keep_new = jnp.exp(maxima - new_high)
        highest = highest.at[start_row:].set(new_high)
        sums = sums.at[start_row:].set(sums[start_row:] * keep_old + totals * keep_new)
        accum = accum.at[start_row:].set(accum[start_row:] * keep_old[..., None] + output * keep_new[..., None])
    attended = (accum / sums[..., None]).reshape(SLABS * GROUP, ATT).astype(jnp.bfloat16)
    projected = jnp.dot(attended, w_out, preferred_element_type=jnp.float32).reshape(SLABS, GROUP, D)
    updated = hidden + modulation[:, 2:3] * projected
    head_in = (layer_norm(updated) * (1.0 + head_mod[:, 1:2]) + head_mod[:, 0:1]).astype(jnp.bfloat16)
    velocity = jnp.dot(head_in.reshape(SLABS * GROUP, D), w_head, preferred_element_type=jnp.float32).reshape(SLABS, GROUP, CHAN)
    table = sigma_table()
    step_size = table[noise_level - 1] - table[noise_level]
    stepped = latents + step_size[:, None, None] * velocity
    return (updated.astype(jnp.bfloat16), jnp.roll(stepped, -1, axis=0))
```

```python
import functools

import jax
import jax.numpy as jnp
from jax import lax
from jax.experimental import pallas as pl
from jax.experimental.pallas import tpu as pltpu
from jax.sharding import PartitionSpec as P

HEADS = 8
HEAD_DIM = 128
LEVELS = 32
TOK_DEV = 48
ATT = 1024
D = 1536
CHAN = 64
PAIR = 2 * HEAD_DIM
LINE = 4
ROWS = LINE * TOK_DEV
BF16 = jnp.bfloat16
F32 = jnp.float32
VMEM_LIMIT = 40 * 1024 * 1024


def from_behind(value, axis, steps):
    count = lax.axis_size(axis)
    pairs = [(source, (source + steps) % count) for source in range(count)]
    return lax.ppermute(value, axis, pairs)


def layer_norm(values):
    center = values - jnp.mean(values, axis=-1, keepdims=True)
    spread = jnp.mean(center * center, axis=-1, keepdims=True)
    return center * lax.rsqrt(spread + 1e-06)


def sigma_table():
    fraction = jnp.arange(LEVELS + 1).astype(jnp.float32) / LEVELS
    return 5.0 * fraction / (1.0 + 4.0 * fraction)


def norm_rope(values, gain_row, position):
    row_count = values.shape[0]
    floats = values.astype(jnp.float32)
    scaled = (
        floats * lax.rsqrt(jnp.mean(floats * floats, axis=-1, keepdims=True) + 1e-06) * gain_row
    )
    halves = HEAD_DIM // 2
    scaled = scaled.reshape(row_count, HEADS, HEAD_DIM)
    frequency = jnp.power(10000.0, -jnp.arange(halves).astype(jnp.float32) / halves)
    angles = position[:, None, None] * frequency[None, None, :]
    cosines = jnp.cos(angles)
    sines = jnp.sin(angles)
    front_half = scaled[..., :halves]
    back_half = scaled[..., halves:]
    turned = jnp.concatenate(
        [front_half * cosines - back_half * sines, front_half * sines + back_half * cosines],
        axis=-1,
    )
    return turned.reshape(row_count, ATT).astype(jnp.bfloat16)


def group_parts(queries, key_rows, value_rows):
    row_count = queries.shape[0]
    key_count = key_rows.shape[0]
    query_heads = queries.reshape(row_count, HEADS, HEAD_DIM).transpose(1, 0, 2)
    key_heads = key_rows.reshape(key_count, HEADS, HEAD_DIM).transpose(1, 0, 2)
    value_heads = value_rows.reshape(key_count, HEADS, HEAD_DIM).transpose(1, 0, 2)

    def one_head(operands):
        query_part, key_part, value_part = operands
        scores = jnp.einsum(
            "rd,kd->rk", query_part, key_part, preferred_element_type=jnp.float32
        ) * HEAD_DIM ** (-0.5)
        maxima = jnp.max(scores, axis=-1)
        weights = jnp.exp(scores - maxima[:, None]).astype(jnp.bfloat16)
        totals = jnp.sum(weights.astype(jnp.float32), axis=-1)
        output = jnp.dot(weights, value_part, preferred_element_type=jnp.float32)
        return (output, maxima, totals)

    output, maxima, totals = lax.map(one_head, (query_heads, key_heads, value_heads))
    return (output.transpose(1, 0, 2).reshape(row_count, ATT), maxima.T, totals.T)


def general(
    stream, latents, time_mod, block_mod, w_qkv, qk_gain, w_out, head_mod, w_head, noise_level
):
    slab_count = lax.axis_size("slab")
    seq_count = lax.axis_size("seq")
    slab_index = lax.axis_index("slab")
    seq_index = lax.axis_index("seq")
    group_rows = TOK_DEV * seq_count
    hidden = stream[0].astype(jnp.float32)
    modulation = block_mod + time_mod[0]
    modded = (layer_norm(hidden) * (1.0 + modulation[1]) + modulation[0]).astype(jnp.bfloat16)
    columns = jnp.dot(
        lax.all_gather(modded, "seq", axis=0, tiled=True), w_qkv, preferred_element_type=jnp.float32
    ).astype(jnp.bfloat16)
    own_position = (slab_index * group_rows + seq_index * TOK_DEV + jnp.arange(TOK_DEV)).astype(
        jnp.float32
    )
    full_mixed = lax.all_gather(columns, "seq", axis=1, tiled=True)
    own_mixed = lax.dynamic_slice_in_dim(full_mixed, seq_index * TOK_DEV, TOK_DEV, 0)
    own_queries = norm_rope(own_mixed[:, :ATT], qk_gain[0], own_position)
    group_position = (slab_index * group_rows + jnp.arange(group_rows)).astype(jnp.float32)
    group_keys = norm_rope(full_mixed[:, ATT : 2 * ATT], qk_gain[1], group_position)
    group_values = full_mixed[:, 2 * ATT :]
    all_queries = lax.all_gather(own_queries[None], "slab", axis=0, tiled=True)
    slab_ids = jnp.arange(slab_count)
    output, maxima, totals = group_parts(
        all_queries.reshape(slab_count * TOK_DEV, ATT), group_keys, group_values
    )
    usable = (slab_ids >= slab_index)[:, None, None]
    output = jnp.where(usable, output.reshape(slab_count, TOK_DEV, ATT), 0.0)
    maxima = jnp.where(usable, maxima.reshape(slab_count, TOK_DEV, HEADS), -1e30)
    totals = jnp.where(usable, totals.reshape(slab_count, TOK_DEV, HEADS), 0.0)
    recv_out, recv_max, recv_sum = (
        lax.all_to_all(output, "slab", split_axis=0, concat_axis=0, tiled=True),
        lax.all_to_all(maxima, "slab", split_axis=0, concat_axis=0, tiled=True),
        lax.all_to_all(totals, "slab", split_axis=0, concat_axis=0, tiled=True),
    )
    highest = jnp.max(recv_max, axis=0)
    weights = jnp.exp(recv_max - highest)
    total_sum = jnp.sum(recv_sum * weights, axis=0)
    accum = jnp.sum(
        recv_out.reshape(slab_count, TOK_DEV, HEADS, HEAD_DIM) * weights[..., None], axis=0
    )
    attended = (accum / total_sum[..., None]).reshape(TOK_DEV, ATT).astype(jnp.bfloat16)
    projected = jnp.dot(attended, w_out, preferred_element_type=jnp.float32)
    updated = hidden + modulation[2] * projected
    head_in = (layer_norm(updated) * (1.0 + head_mod[0, 1]) + head_mod[0, 0]).astype(jnp.bfloat16)
    velocity = jnp.dot(head_in, w_head, preferred_element_type=jnp.float32)
    table = sigma_table()
    level_ids = jnp.arange(LEVELS + 1)
    current_level = noise_level[0]
    sigma_now = jnp.sum(jnp.where(level_ids == current_level, table, 0.0))
    sigma_next = jnp.sum(jnp.where(level_ids == current_level - 1, table, 0.0))
    stepped = latents[0] + (sigma_next - sigma_now) * velocity
    moved = from_behind(stepped[None], "slab", -1)
    return (updated.astype(jnp.bfloat16)[None], moved)


def vmem_call(kernel, outs, name, flops, scratch=()):
    whole = pl.BlockSpec(memory_space=pltpu.VMEM)

    def call(scalars, *operands):
        return pl.pallas_call(
            kernel,
            out_shape=[jax.ShapeDtypeStruct(shape, dtype) for shape, dtype in outs],
            in_specs=[pl.BlockSpec(memory_space=pltpu.SMEM)] + [whole] * len(operands),
            out_specs=[whole] * len(outs),
            scratch_shapes=list(scratch),
            compiler_params=pltpu.CompilerParams(vmem_limit_bytes=VMEM_LIMIT),
            cost_estimate=pl.CostEstimate(flops=flops, bytes_accessed=1 << 20, transcendentals=0),
            name=name,
        )(scalars, *operands)

    return call


def dot_rows(left, right):
    return lax.dot_general(left, right, (((1,), (1,)), ((), ())), preferred_element_type=F32)


def project_kernel(
    place, x0, x1, x2, x3, time_mod, block_mod, w_own, w_first, w_second,
    near_out, far_out, keep_out, sums_out, modded, mixed,
):
    line, side, core = place[0], place[1], place[2]
    modulation = block_mod[...] + time_mod[...]
    shift, scale = modulation[0:1], 1.0 + modulation[1:2]
    for step, rows in enumerate((x0, x1, x2, x3)):
        normal = layer_norm(rows[...].astype(F32))
        at = pl.multiple_of(jnp.bitwise_xor(line, step) * TOK_DEV, 16)
        modded[pl.ds(at, TOK_DEV), :] = (normal * scale + shift).astype(BF16)
    half = D // 2
    width = w_own.shape[1]
    own = jnp.dot(modded[...], w_own[...], preferred_element_type=F32)
    other = jnp.dot(
        modded[:, pl.ds(pl.multiple_of(core * half, half), half)], w_first[...],
        preferred_element_type=F32,
    )
    other += jnp.dot(
        modded[:, pl.ds(pl.multiple_of((1 - core) * half, half), half)], w_second[...],
        preferred_element_type=F32,
    )
    mixed[:, pl.ds(pl.multiple_of(side * width, width), width)] = own.astype(BF16)
    mixed[:, pl.ds(pl.multiple_of((1 - side) * width, width), width)] = other.astype(BF16)
    ones = jnp.ones((16, PAIR), BF16)
    row_id = lax.broadcasted_iota(jnp.int32, (16, ROWS), 0)
    picked = jnp.zeros((16, ROWS), F32)
    for unit in range(3):
        values = mixed[:, unit * PAIR : (unit + 1) * PAIR].astype(F32)
        squares = values * values
        high = squares.astype(BF16)
        low = (squares - high.astype(F32)).astype(BF16)
        total = dot_rows(ones, high) + dot_rows(ones, low)
        kind = (line * 3 + unit) // LINE
        picked += jnp.where(row_id // 3 == kind, total, 0.0)
    picked = jnp.where(row_id < 6, picked, 0.0)
    first = picked.astype(BF16).astype(F32)
    second = (picked - first).astype(BF16).astype(F32)
    third = picked - first - second
    part = row_id % 3
    packed = jnp.where(part == 0, first, jnp.where(part == 1, second, third)).astype(BF16)
    padded = jnp.concatenate([packed, jnp.zeros((16, PAIR - ROWS), BF16)], axis=1)
    sums_out[...] = padded
    near_out[:ROWS, :] = mixed[:, PAIR : 2 * PAIR]
    near_out[ROWS:, :] = padded
    odd = line % 2
    at = pl.multiple_of((1 - odd) * 2 * PAIR, PAIR)
    far_out[:ROWS, :] = mixed[:, pl.ds(at, PAIR)]
    far_out[ROWS:, :] = padded
    at = pl.multiple_of(odd * 2 * PAIR, PAIR)
    keep_out[...] = mixed[:, pl.ds(at, PAIR)]


def rope_kernel(
    place, keep, near, far, own_sums, last_sums, gains, cosines, sines, q_out, kv_out, units
):
    line = place[0]
    units[0] = keep[...]
    units[1] = near[:ROWS, :]
    units[2] = far[:ROWS, :]
    pieces = [
        own_sums[...].astype(F32), near[ROWS:, :].astype(F32),
        far[ROWS:, :].astype(F32), last_sums[...].astype(F32),
    ]
    row_id = lax.broadcasted_iota(jnp.int32, (16, 1), 0)
    cos, sin = cosines[...], sines[...]
    for kind in range(2):
        wanted = row_id // 3 == kind
        total = jnp.zeros((1, PAIR), F32)
        for piece in pieces:
            total += jnp.sum(jnp.where(wanted, piece, 0.0), axis=0, keepdims=True)
        scale = lax.rsqrt(total * (1.0 / ATT) + 1e-06)
        scale = jnp.transpose(jnp.broadcast_to(scale, (HEAD_DIM, PAIR)))[:ROWS]
        values = units[place[3 + kind]].astype(F32)
        for head in range(2):
            columns = slice(head * HEAD_DIM, (head + 1) * HEAD_DIM)
            at = pl.multiple_of(line * PAIR + head * HEAD_DIM, HEAD_DIM)
            scaled = values[:, columns] * scale * gains[kind : kind + 1, pl.ds(at, HEAD_DIM)]
            turned = scaled * cos + pltpu.roll(scaled, HEAD_DIM // 2, axis=1) * sin
            (kv_out if kind else q_out)[:, columns] = turned.astype(BF16)
    kv_out[:, PAIR:] = units[place[5]]


def attend_kernel(
    place, queries, a0, a1, b0, b1, c0, c1, d0, d1, o0, o1, o2, o3, result, accum, highest, sums
):
    line = place[0]
    accum[...] = jnp.zeros_like(accum)
    sums[...] = jnp.zeros_like(sums)
    highest[...] = jnp.full_like(highest, -1e30)

    def group(one, two):
        for head in range(2):
            columns = slice(head * HEAD_DIM, (head + 1) * HEAD_DIM)
            value_columns = slice(PAIR + head * HEAD_DIM, PAIR + (head + 1) * HEAD_DIM)
            keys = jnp.concatenate([one[:, columns], two[:, columns]], axis=0)
            values = jnp.concatenate([one[:, value_columns], two[:, value_columns]], axis=0)
            scores = dot_rows(queries[:, columns], keys) * HEAD_DIM ** (-0.5)
            maxima = jnp.max(scores, axis=-1, keepdims=True)
            weights = jnp.exp(scores - maxima).astype(BF16)
            totals = jnp.sum(weights.astype(F32), axis=-1, keepdims=True)
            output = jnp.dot(weights, values, preferred_element_type=F32)
            old = highest[head]
            new = jnp.maximum(old, maxima)
            keep_old, keep_new = jnp.exp(old - new), jnp.exp(maxima - new)
            highest[head] = new
            sums[head] = sums[head] * keep_old + totals * keep_new
            accum[head] = accum[head] * keep_old + output * keep_new

    group(a0, a1)
    pl.when(place[2] == 1)(lambda: group(b0, b1))
    pl.when(place[6] == 1)(lambda: group(c0, c1))
    pl.when(place[6] == 1)(lambda: group(d0, d1))
    for head in range(2):
        columns = slice(head * HEAD_DIM, (head + 1) * HEAD_DIM)
        result[:, columns] = (accum[head] / sums[head]).astype(BF16)
    for step, out in enumerate((o0, o1, o2, o3)):
        at = pl.multiple_of(jnp.bitwise_xor(line, step) * TOK_DEV, 16)
        out[...] = result[pl.ds(at, TOK_DEV), :]


def finish_kernel(
    place, r0, r1, r2, r3, w_out, stream, time_mod, block_mod, head_mod, w_head, latents,
    stream_out, latents_out,
):
    line = place[0]
    projected = jnp.zeros((TOK_DEV, D), F32)
    for step, rows in enumerate((r0, r1, r2, r3)):
        at = pl.multiple_of(jnp.bitwise_xor(line, step) * PAIR, PAIR)
        projected += jnp.dot(rows[...], w_out[pl.ds(at, PAIR), :], preferred_element_type=F32)
    gate = block_mod[2:3] + time_mod[2:3]
    updated = stream[...].astype(F32) + gate * projected
    stream_out[...] = updated.astype(BF16)
    head_in = (layer_norm(updated) * (1.0 + head_mod[1:2]) + head_mod[0:1]).astype(BF16)
    velocity = jnp.dot(head_in, w_head[...], preferred_element_type=F32)

    def sigma(level):
        fraction = jnp.full((1, CHAN), level, jnp.int32).astype(F32) / LEVELS
        return 5.0 * fraction / (1.0 + 4.0 * fraction)

    latents_out[...] = latents[...] + (sigma(place[7] - 1) - sigma(place[7])) * velocity


def lines(
    stream, latents, time_mod, block_mod, w_qkv, qk_gain, w_out, head_mod, w_head, noise_level
):
    slab, seq = lax.axis_index("slab"), lax.axis_index("seq")
    line, side, core = seq // 2, seq % 2, slab % 2
    slots = jnp.array([[0, 1, 2], [1, 0, 2], [2, 0, 1], [2, 1, 0]], jnp.int32)[line]
    place = jnp.concatenate(
        [jnp.stack([line, side, core]), slots, (slab // 2)[None], noise_level]
    ).astype(jnp.int32)

    def along(step, value):
        return lax.ppermute(value, "seq", [(i, i ^ (2 * step)) for i in range(2 * LINE)])

    def across(value):
        return lax.ppermute(value, "seq", [(i, i ^ 1) for i in range(2 * LINE)])

    def cores(value):
        return lax.ppermute(value, "slab", [(i, i ^ 1) for i in range(4)])

    def chips(value, flip):
        count = 2 * LINE
        pairs = [(s * count + i, (s + 2) * count + (i ^ flip)) for s in range(2) for i in range(count)]
        return lax.ppermute(value, ("slab", "seq"), pairs)

    rows = stream[0]
    w_first = across(lax.dynamic_slice_in_dim(w_qkv, core * (D // 2), D // 2, 0))
    x3, x2, x1 = along(3, rows), along(2, rows), along(1, rows)
    w_second = cores(w_first)

    at = (jnp.arange(LINE)[:, None] * 2 + side) * TOK_DEV + jnp.arange(TOK_DEV)[None]
    position = (slab * (2 * LINE * TOK_DEV) + at.reshape(ROWS)).astype(F32)
    halves = HEAD_DIM // 2
    frequency = jnp.power(10000.0, -jnp.arange(halves).astype(F32) / halves)
    angles = position[:, None] * frequency[None]
    cosines, sines = jnp.cos(angles), jnp.sin(angles)
    cosines = jnp.concatenate([cosines, cosines], axis=1)
    sines = jnp.concatenate([-sines, sines], axis=1)

    message = (ROWS + 16, PAIR)
    near, far, keep, sums = vmem_call(
        project_kernel,
        [(message, BF16), (message, BF16), ((ROWS, PAIR), BF16), ((16, PAIR), BF16)],
        "project", 2 * ROWS * D * 3 * PAIR,
        [pltpu.VMEM((ROWS, D), BF16), pltpu.VMEM((ROWS, 3 * PAIR), BF16)],
    )(place, rows, x1, x2, x3, time_mod[0], block_mod, w_qkv, w_first, w_second)
    far, near, last_sums = along(2, far), along(1, near), along(3, sums)
    queries, pairs = vmem_call(
        rope_kernel,
        [((ROWS, PAIR), BF16), ((ROWS, 2 * PAIR), BF16)],
        "rope", 1 << 22, [pltpu.VMEM((3, ROWS, PAIR), BF16)],
    )(place, keep, near, far, sums, last_sums, qk_gain, cosines, sines)
    core_pairs = cores(pairs)
    side_pairs = across(pairs)
    chip_pairs = chips(pairs, 0)
    both_pairs = chips(pairs, 1)
    shape, dtype = (TOK_DEV, PAIR), BF16
    state = pltpu.VMEM((2, ROWS, 1), F32)
    parts = vmem_call(
        attend_kernel, [(shape, dtype)] * 4, "attend", 1 << 28,
        [pltpu.VMEM((ROWS, PAIR), BF16), pltpu.VMEM((2, ROWS, HEAD_DIM), F32), state, state],
    )(
        place, queries, pairs, side_pairs, core_pairs, cores(side_pairs),
        chip_pairs, both_pairs, cores(chip_pairs), cores(both_pairs),
    )
    taken = [parts[0]] + [along(step, parts[step]) for step in (1, 2, 3)]
    new_stream, stepped = vmem_call(
        finish_kernel, [((TOK_DEV, D), BF16), ((TOK_DEV, CHAN), F32)], "finish", 1 << 28
    )(place, *taken, w_out, rows, time_mod[0], block_mod, head_mod[0], w_head, latents[0])
    return (new_stream[None], from_behind(stepped[None], "slab", -1))


def solution(mesh):
    in_specs = (
        P("slab", "seq", None),
        P("slab", "seq", None),
        P("slab", None, None),
        P(),
        P(None, "seq"),
        P(),
        P(),
        P("slab", None, None),
        P(),
        P("slab"),
    )
    out_specs = (P("slab", "seq", None), P("slab", "seq", None))
    local = lines if tuple(mesh.shape.values()) == (4, 2 * LINE) else general
    return jax.shard_map(local, mesh=mesh, in_specs=in_specs, out_specs=out_specs, check_vma=False)
```

```python
import functools

import jax
import jax.numpy as jnp
from jax import lax
from jax.experimental import pallas as pl
from jax.experimental.pallas import tpu as pltpu
from jax.sharding import PartitionSpec as P

HEADS = 8
HEAD_DIM = 128
LEVELS = 32
TOK_DEV = 48
ATT = 1024
D = 1536
CHAN = 64
PAIR = 2 * HEAD_DIM
LINE = 4
ROWS = LINE * TOK_DEV
BF16 = jnp.bfloat16
F32 = jnp.float32
VMEM_LIMIT = 40 * 1024 * 1024


def from_behind(value, axis, steps):
    count = lax.axis_size(axis)
    pairs = [(source, (source + steps) % count) for source in range(count)]
    return lax.ppermute(value, axis, pairs)


def layer_norm(values):
    center = values - jnp.mean(values, axis=-1, keepdims=True)
    spread = jnp.mean(center * center, axis=-1, keepdims=True)
    return center * lax.rsqrt(spread + 1e-06)


def sigma_table():
    fraction = jnp.arange(LEVELS + 1).astype(jnp.float32) / LEVELS
    return 5.0 * fraction / (1.0 + 4.0 * fraction)


def norm_rope(values, gain_row, position):
    row_count = values.shape[0]
    floats = values.astype(jnp.float32)
    scaled = (
        floats * lax.rsqrt(jnp.mean(floats * floats, axis=-1, keepdims=True) + 1e-06) * gain_row
    )
    halves = HEAD_DIM // 2
    scaled = scaled.reshape(row_count, HEADS, HEAD_DIM)
    frequency = jnp.power(10000.0, -jnp.arange(halves).astype(jnp.float32) / halves)
    angles = position[:, None, None] * frequency[None, None, :]
    cosines = jnp.cos(angles)
    sines = jnp.sin(angles)
    front_half = scaled[..., :halves]
    back_half = scaled[..., halves:]
    turned = jnp.concatenate(
        [front_half * cosines - back_half * sines, front_half * sines + back_half * cosines],
        axis=-1,
    )
    return turned.reshape(row_count, ATT).astype(jnp.bfloat16)


def group_parts(queries, key_rows, value_rows):
    row_count = queries.shape[0]
    key_count = key_rows.shape[0]
    query_heads = queries.reshape(row_count, HEADS, HEAD_DIM).transpose(1, 0, 2)
    key_heads = key_rows.reshape(key_count, HEADS, HEAD_DIM).transpose(1, 0, 2)
    value_heads = value_rows.reshape(key_count, HEADS, HEAD_DIM).transpose(1, 0, 2)

    def one_head(operands):
        query_part, key_part, value_part = operands
        scores = jnp.einsum(
            "rd,kd->rk", query_part, key_part, preferred_element_type=jnp.float32
        ) * HEAD_DIM ** (-0.5)
        maxima = jnp.max(scores, axis=-1)
        weights = jnp.exp(scores - maxima[:, None]).astype(jnp.bfloat16)
        totals = jnp.sum(weights.astype(jnp.float32), axis=-1)
        output = jnp.dot(weights, value_part, preferred_element_type=jnp.float32)
        return (output, maxima, totals)

    output, maxima, totals = lax.map(one_head, (query_heads, key_heads, value_heads))
    return (output.transpose(1, 0, 2).reshape(row_count, ATT), maxima.T, totals.T)


def general(
    stream, latents, time_mod, block_mod, w_qkv, qk_gain, w_out, head_mod, w_head, noise_level
):
    slab_count = lax.axis_size("slab")
    seq_count = lax.axis_size("seq")
    slab_index = lax.axis_index("slab")
    seq_index = lax.axis_index("seq")
    group_rows = TOK_DEV * seq_count
    hidden = stream[0].astype(jnp.float32)
    modulation = block_mod + time_mod[0]
    modded = (layer_norm(hidden) * (1.0 + modulation[1]) + modulation[0]).astype(jnp.bfloat16)
    columns = jnp.dot(
        lax.all_gather(modded, "seq", axis=0, tiled=True), w_qkv, preferred_element_type=jnp.float32
    ).astype(jnp.bfloat16)
    own_position = (slab_index * group_rows + seq_index * TOK_DEV + jnp.arange(TOK_DEV)).astype(
        jnp.float32
    )
    full_mixed = lax.all_gather(columns, "seq", axis=1, tiled=True)
    own_mixed = lax.dynamic_slice_in_dim(full_mixed, seq_index * TOK_DEV, TOK_DEV, 0)
    own_queries = norm_rope(own_mixed[:, :ATT], qk_gain[0], own_position)
    group_position = (slab_index * group_rows + jnp.arange(group_rows)).astype(jnp.float32)
    group_keys = norm_rope(full_mixed[:, ATT : 2 * ATT], qk_gain[1], group_position)
    group_values = full_mixed[:, 2 * ATT :]
    all_queries = lax.all_gather(own_queries[None], "slab", axis=0, tiled=True)
    slab_ids = jnp.arange(slab_count)
    output, maxima, totals = group_parts(
        all_queries.reshape(slab_count * TOK_DEV, ATT), group_keys, group_values
    )
    usable = (slab_ids >= slab_index)[:, None, None]
    output = jnp.where(usable, output.reshape(slab_count, TOK_DEV, ATT), 0.0)
    maxima = jnp.where(usable, maxima.reshape(slab_count, TOK_DEV, HEADS), -1e30)
    totals = jnp.where(usable, totals.reshape(slab_count, TOK_DEV, HEADS), 0.0)
    recv_out, recv_max, recv_sum = (
        lax.all_to_all(output, "slab", split_axis=0, concat_axis=0, tiled=True),
        lax.all_to_all(maxima, "slab", split_axis=0, concat_axis=0, tiled=True),
        lax.all_to_all(totals, "slab", split_axis=0, concat_axis=0, tiled=True),
    )
    highest = jnp.max(recv_max, axis=0)
    weights = jnp.exp(recv_max - highest)
    total_sum = jnp.sum(recv_sum * weights, axis=0)
    accum = jnp.sum(
        recv_out.reshape(slab_count, TOK_DEV, HEADS, HEAD_DIM) * weights[..., None], axis=0
    )
    attended = (accum / total_sum[..., None]).reshape(TOK_DEV, ATT).astype(jnp.bfloat16)
    projected = jnp.dot(attended, w_out, preferred_element_type=jnp.float32)
    updated = hidden + modulation[2] * projected
    head_in = (layer_norm(updated) * (1.0 + head_mod[0, 1]) + head_mod[0, 0]).astype(jnp.bfloat16)
    velocity = jnp.dot(head_in, w_head, preferred_element_type=jnp.float32)
    table = sigma_table()
    level_ids = jnp.arange(LEVELS + 1)
    current_level = noise_level[0]
    sigma_now = jnp.sum(jnp.where(level_ids == current_level, table, 0.0))
    sigma_next = jnp.sum(jnp.where(level_ids == current_level - 1, table, 0.0))
    stepped = latents[0] + (sigma_next - sigma_now) * velocity
    moved = from_behind(stepped[None], "slab", -1)
    return (updated.astype(jnp.bfloat16)[None], moved)


def vmem_call(kernel, outs, name, flops, scratch=(), placed=0):
    whole = pl.BlockSpec(memory_space=pltpu.VMEM)
    stay = pl.BlockSpec(memory_space=pltpu.HBM)

    def call(*operands):
        return pl.pallas_call(
            kernel,
            out_shape=[jax.ShapeDtypeStruct(shape, dtype) for shape, dtype in outs],
            in_specs=[whole] * (len(operands) - placed) + [stay] * placed,
            out_specs=[whole] * len(outs),
            scratch_shapes=list(scratch),
            compiler_params=pltpu.CompilerParams(vmem_limit_bytes=VMEM_LIMIT),
            cost_estimate=pl.CostEstimate(flops=flops, bytes_accessed=1 << 20, transcendentals=0),
            name=name,
        )(*operands)

    return call


def here():
    slab, seq = lax.axis_index("slab"), lax.axis_index("seq")
    return seq // 2, seq % 2, slab % 2, slab // 2


def dot_rows(left, right):
    return lax.dot_general(left, right, (((1,), (1,)), ((), ())), preferred_element_type=F32)


def modulated(rows, time_mod, block_mod):
    shift = block_mod[0:1] + time_mod[0]
    scale = 1.0 + (block_mod[1:2] + time_mod[1])
    return (layer_norm(rows[...].astype(F32)) * scale + shift).astype(BF16)


def own_kernel(x1, x2, time_mod, block_mod, w_own, modded, own):
    for step, rows in enumerate((x1, x2)):
        modded[step * TOK_DEV : (step + 1) * TOK_DEV, :] = modulated(rows, time_mod, block_mod)
    own[...] = jnp.dot(modded[...], w_own[...], preferred_element_type=F32).astype(BF16)


def project_kernel(
    x3, x0, time_mod, block_mod, w_own, w_first, w_second, modded_in, own_in,
    far_out, near_out, keep_out, sums_out, modded, mixed,
):
    line, side, core, _ = here()
    half = D // 2
    width = w_own.shape[1]
    modded[:TOK_DEV, :] = modulated(x0, time_mod, block_mod)
    modded[TOK_DEV : 2 * TOK_DEV, :] = modulated(x3, time_mod, block_mod)
    modded[2 * TOK_DEV :, :] = modded_in[...]
    late = jnp.dot(modded[: 2 * TOK_DEV, :], w_own[...], preferred_element_type=F32).astype(BF16)
    other = jnp.dot(
        modded[:, pl.ds(pl.multiple_of(core * half, half), half)], w_first[...],
        preferred_element_type=F32,
    )
    other += jnp.dot(
        modded[:, pl.ds(pl.multiple_of((1 - core) * half, half), half)], w_second[...],
        preferred_element_type=F32,
    )
    other = other.astype(BF16)
    mine = pl.multiple_of(side * width, width)
    there = pl.multiple_of((1 - side) * width, width)
    for place, step in enumerate((0, 3, 1, 2)):
        at = pl.multiple_of(jnp.bitwise_xor(line, step) * TOK_DEV, 16)
        rows = slice(place * TOK_DEV, (place + 1) * TOK_DEV)
        if place < 2:
            mixed[pl.ds(at, TOK_DEV), pl.ds(mine, width)] = late[rows]
        else:
            behind = slice((place - 2) * TOK_DEV, (place - 1) * TOK_DEV)
            mixed[pl.ds(at, TOK_DEV), pl.ds(mine, width)] = own_in[behind, :]
        mixed[pl.ds(at, TOK_DEV), pl.ds(there, width)] = other[rows]
    ones = jnp.ones((16, PAIR), BF16)
    row_id = lax.broadcasted_iota(jnp.int32, (16, ROWS), 0)
    picked = jnp.zeros((16, ROWS), F32)
    for unit in range(3):
        values = mixed[:, unit * PAIR : (unit + 1) * PAIR].astype(F32)
        squares = values * values
        high = squares.astype(BF16)
        low = (squares - high.astype(F32)).astype(BF16)
        total = dot_rows(ones, high) + dot_rows(ones, low)
        kind = (line * 3 + unit) // LINE
        picked += jnp.where(row_id // 3 == kind, total, 0.0)
    picked = jnp.where(row_id < 6, picked, 0.0)
    first = picked.astype(BF16).astype(F32)
    second = (picked - first).astype(BF16).astype(F32)
    third = picked - first - second
    part = row_id % 3
    packed = jnp.where(part == 0, first, jnp.where(part == 1, second, third)).astype(BF16)
    padded = jnp.concatenate([packed, jnp.zeros((16, PAIR - ROWS), BF16)], axis=1)
    sums_out[...] = padded
    near_out[:ROWS, :] = mixed[:, PAIR : 2 * PAIR]
    near_out[ROWS:, :] = padded
    odd = line % 2
    at = pl.multiple_of((1 - odd) * 2 * PAIR, PAIR)
    far_out[:ROWS, :] = mixed[:, pl.ds(at, PAIR)]
    far_out[ROWS:, :] = padded
    at = pl.multiple_of(odd * 2 * PAIR, PAIR)
    keep_out[...] = mixed[:, pl.ds(at, PAIR)]


def rope_kernel(
    far, last_sums, near, keep, own_sums, gains, cosines, sines, q_out, kv_out, units
):
    line, _, _, _ = here()
    upper, odd = line // 2, line % 2
    slots = (
        jnp.where(upper == 1, 2, odd),
        jnp.where((line == 0) | (line == 3), 1, 0),
        jnp.where(upper == 0, 2, 1 - odd),
    )
    units[0] = keep[...]
    units[1] = near[:ROWS, :]
    units[2] = far[:ROWS, :]
    pieces = [
        own_sums[...].astype(F32), near[ROWS:, :].astype(F32),
        far[ROWS:, :].astype(F32), last_sums[...].astype(F32),
    ]
    row_id = lax.broadcasted_iota(jnp.int32, (16, 1), 0)
    cos, sin = cosines[...], sines[...]
    for kind in range(2):
        wanted = row_id // 3 == kind
        total = jnp.zeros((1, PAIR), F32)
        for piece in pieces:
            total += jnp.sum(jnp.where(wanted, piece, 0.0), axis=0, keepdims=True)
        scale = lax.rsqrt(total * (1.0 / ATT) + 1e-06)
        scale = jnp.transpose(jnp.broadcast_to(scale, (HEAD_DIM, PAIR)))[:ROWS]
        values = units[slots[kind]].astype(F32)
        for head in range(2):
            columns = slice(head * HEAD_DIM, (head + 1) * HEAD_DIM)
            at = pl.multiple_of(line * PAIR + head * HEAD_DIM, HEAD_DIM)
            scaled = values[:, columns] * scale * gains[kind : kind + 1, pl.ds(at, HEAD_DIM)]
            turned = scaled * cos + pltpu.roll(scaled, HEAD_DIM // 2, axis=1) * sin
            (kv_out if kind else q_out)[:, columns] = turned.astype(BF16)
    kv_out[:, PAIR:] = units[slots[2]]


def attend_group(queries, one, two, state):
    total, highest = state
    ones = jnp.ones((2 * ROWS, HEAD_DIM), BF16)
    for head in range(2):
        columns = slice(head * HEAD_DIM, (head + 1) * HEAD_DIM)
        value_columns = slice(PAIR + head * HEAD_DIM, PAIR + (head + 1) * HEAD_DIM)
        keys = jnp.concatenate([one[:, columns], two[:, columns]], axis=0)
        values = jnp.concatenate([one[:, value_columns], two[:, value_columns]], axis=0)
        scores = dot_rows(queries[:, columns], keys) * HEAD_DIM ** (-0.5)
        maxima = jnp.max(scores, axis=-1, keepdims=True)
        weights = jnp.exp(scores - maxima).astype(BF16)
        output = jnp.dot(
            weights, jnp.concatenate([values, ones], axis=1), preferred_element_type=F32
        )
        old = highest[head]
        new = jnp.maximum(old, maxima)
        keep_old, keep_new = jnp.exp(old - new), jnp.exp(maxima - new)
        highest[head] = new
        for part in range(2):
            lanes = slice(part * HEAD_DIM, (part + 1) * HEAD_DIM)
            total[head, :, lanes] = total[head, :, lanes] * keep_old + output[:, lanes] * keep_new


def own_attend_kernel(queries, a0, a1, total, highest):
    total[...] = jnp.zeros_like(total)
    highest[...] = jnp.full_like(highest, -1e30)
    attend_group(queries, a0, a1, (total, highest))


def next_attend_kernel(which, queries, one, two, total_in, highest_in, total, highest):
    total[...] = total_in[...]
    highest[...] = highest_in[...]
    pl.when(here()[which] == 1)(lambda: attend_group(queries, one, two, (total, highest)))


def last_attend_kernel(
    queries, d0, d1, total_in, highest_in, o3, o2, o1, o0, total, highest, result
):
    line, _, _, chip = here()
    total[...] = total_in[...]
    highest[...] = highest_in[...]
    pl.when(chip == 1)(lambda: attend_group(queries, d0, d1, (total, highest)))
    for head in range(2):
        columns = slice(head * HEAD_DIM, (head + 1) * HEAD_DIM)
        result[:, columns] = (total[head, :, :HEAD_DIM] / total[head, :, HEAD_DIM:]).astype(BF16)
    for step, out in enumerate((o0, o1, o2, o3)):
        at = pl.multiple_of(jnp.bitwise_xor(line, step) * TOK_DEV, 16)
        out[...] = result[pl.ds(at, TOK_DEV), :]


def load(sources, held, arrived):
    copies = [
        pltpu.make_async_copy(source, target, arrived.at[i])
        for i, (source, target) in enumerate(zip(sources, held))
    ]
    for copy in copies:
        copy.start()
    return copies


def times_w_out(rows, w_out, step):
    at = pl.multiple_of(jnp.bitwise_xor(here()[0], step) * PAIR, PAIR)
    return jnp.dot(rows[...], w_out[pl.ds(at, PAIR), :], preferred_element_type=F32)


def begin_kernel(
    r0, w_out, stream_in, time_in, block_in, head_in, base, vectors,
    stream, time_mod, block_mod, head_mod, arrived,
):
    copies = load(
        (stream_in, time_in, block_in, head_in), (stream, time_mod, block_mod, head_mod), arrived
    )
    projected = times_w_out(r0, w_out, 0)
    for copy in copies:
        copy.wait()
    gate = block_mod[2:3] + time_mod[2]
    base[...] = stream[...].astype(F32) + gate * projected
    vectors[0:1] = gate
    vectors[1:2] = 1.0 + head_mod[1:2]
    vectors[2:3] = head_mod[0:1]


def finish_kernel(
    r3, r2, r1, w_out, base, vectors, w_head, levels, latents_in, stream_out, latents_out,
    latents, arrived,
):
    copies = load((latents_in,), (latents,), arrived)
    projected = times_w_out(r3, w_out, 3) + times_w_out(r2, w_out, 2) + times_w_out(r1, w_out, 1)
    updated = base[...] + vectors[0:1] * projected
    stream_out[...] = updated.astype(BF16)
    head_in = (layer_norm(updated) * vectors[1:2] + vectors[2:3]).astype(BF16)
    velocity = dot_rows(head_in, w_head[...])

    def sigma(level):
        fraction = level.astype(F32) / LEVELS
        return 5.0 * fraction / (1.0 + 4.0 * fraction)

    level = levels[...]
    copies[0].wait()
    latents_out[...] = latents[...] + (sigma(level - 1) - sigma(level)) * velocity


def lines(
    stream, latents, time_mod, block_mod, w_qkv, qk_gain, w_out, head_mod, w_head, noise_level
):
    slab, seq = lax.axis_index("slab"), lax.axis_index("seq")
    side, core = seq % 2, slab % 2

    def along(step, value):
        return lax.ppermute(value, "seq", [(i, i ^ (2 * step)) for i in range(2 * LINE)])

    def across(value):
        return lax.ppermute(value, "seq", [(i, i ^ 1) for i in range(2 * LINE)])

    def cores(value):
        return lax.ppermute(value, "slab", [(i, i ^ 1) for i in range(4)])

    def chips(value, flip):
        count = 2 * LINE
        pairs = [(s * count + i, (s + 2) * count + (i ^ flip)) for s in range(2) for i in range(count)]
        return lax.ppermute(value, ("slab", "seq"), pairs)

    rows = stream[0]
    time_rows = time_mod.transpose(1, 0, 2)
    w_first = across(lax.dynamic_slice_in_dim(w_qkv, core * (D // 2), D // 2, 0))
    x3, x2, x1 = along(3, rows), along(2, rows), along(1, rows)
    at = (jnp.arange(LINE)[:, None] * 2 + side) * TOK_DEV + jnp.arange(TOK_DEV)[None]
    position = (slab * (2 * LINE * TOK_DEV) + at.reshape(ROWS)).astype(F32)
    halves = HEAD_DIM // 2
    frequency = jnp.power(10000.0, -jnp.arange(halves).astype(F32) / halves)
    angles = position[:, None] * frequency[None]
    cosines, sines = jnp.cos(angles), jnp.sin(angles)
    cosines = jnp.concatenate([cosines, cosines], axis=1)
    sines = jnp.concatenate([-sines, sines], axis=1)

    width = w_qkv.shape[1]
    modded, own = vmem_call(
        own_kernel, [((2 * TOK_DEV, D), BF16), ((2 * TOK_DEV, width), BF16)], "own", 1 << 28
    )(x1, x2, time_rows, block_mod, w_qkv)
    w_second = cores(w_first)
    message = (ROWS + 16, PAIR)
    far, near, keep, sums = vmem_call(
        project_kernel,
        [(message, BF16), (message, BF16), ((ROWS, PAIR), BF16), ((16, PAIR), BF16)],
        "project", 1 << 28,
        [pltpu.VMEM((ROWS, D), BF16), pltpu.VMEM((ROWS, 3 * PAIR), BF16)],
    )(x3, rows, time_rows, block_mod, w_qkv, w_first, w_second, modded, own)
    far, last_sums, near = along(2, far), along(3, sums), along(1, near)
    queries, pairs = vmem_call(
        rope_kernel,
        [((ROWS, PAIR), BF16), ((ROWS, 2 * PAIR), BF16)],
        "rope", 1 << 22, [pltpu.VMEM((3, ROWS, PAIR), BF16)],
    )(far, last_sums, near, keep, sums, qk_gain, cosines, sines)
    chip_pairs, both_pairs = chips(pairs, 0), chips(pairs, 1)
    side_pairs, core_pairs = across(pairs), cores(pairs)
    state = [((2, ROWS, PAIR), F32), ((2, ROWS, HEAD_DIM), F32)]
    held = [pltpu.VMEM(shape, dtype) for shape, dtype in state]
    now = vmem_call(own_attend_kernel, state, "attend_own", 1 << 27)(queries, pairs, side_pairs)
    now, chip_pairs, both_pairs, side_pairs = lax.optimization_barrier(
        (now, chip_pairs, both_pairs, side_pairs)
    )
    core_side, core_chip, core_both = cores(side_pairs), cores(chip_pairs), cores(both_pairs)
    for name, which, blocks in (
        ("attend_core", 2, (core_pairs, core_side)),
        ("attend_chip", 3, (chip_pairs, both_pairs)),
    ):
        kernel = functools.partial(next_attend_kernel, which)
        now = vmem_call(kernel, state, name, 1 << 27)(queries, *blocks, *now)
    part3, part2, part1, part0 = vmem_call(
        last_attend_kernel, [((TOK_DEV, PAIR), BF16)] * 4, "attend_last", 1 << 27,
        held + [pltpu.VMEM((ROWS, PAIR), BF16)],
    )(queries, core_chip, core_both, *now)
    late = [along(3, part3), along(2, part2), along(1, part1)]
    loaded = (rows, time_rows, block_mod, head_mod[0])
    base, vectors = vmem_call(
        begin_kernel, [((TOK_DEV, D), F32), ((8, D), F32)], "begin", 1 << 28,
        [pltpu.VMEM(v.shape, v.dtype) for v in loaded] + [pltpu.SemaphoreType.DMA((len(loaded),))],
        placed=len(loaded),
    )(part0, w_out, *loaded)
    level = jnp.broadcast_to(noise_level[:, None], (1, CHAN))
    new_stream, stepped = vmem_call(
        finish_kernel, [((TOK_DEV, D), BF16), ((TOK_DEV, CHAN), F32)], "finish", 1 << 28,
        [pltpu.VMEM((TOK_DEV, CHAN), F32), pltpu.SemaphoreType.DMA((1,))], placed=1,
    )(*late, w_out, base, vectors, w_head.T, level, latents[0])
    return (new_stream[None], from_behind(stepped[None], "slab", -1))


def solution(mesh):
    in_specs = (
        P("slab", "seq", None),
        P("slab", "seq", None),
        P("slab", None, None),
        P(),
        P(None, "seq"),
        P(),
        P(),
        P("slab", None, None),
        P(),
        P("slab"),
    )
    out_specs = (P("slab", "seq", None), P("slab", "seq", None))
    local = lines if tuple(mesh.shape.values()) == (4, 2 * LINE) else general
    return jax.shard_map(local, mesh=mesh, in_specs=in_specs, out_specs=out_specs, check_vma=False)
```

```python
import functools

import jax
import jax.numpy as jnp
from jax import lax
from jax.experimental import pallas as pl
from jax.experimental.pallas import tpu as pltpu
from jax.sharding import PartitionSpec as P

HEADS = 8
HEAD_DIM = 128
LEVELS = 32
TOK_DEV = 48
ATT = 1024
D = 1536
CHAN = 64
PAIR = 2 * HEAD_DIM
LINE = 4
ROWS = LINE * TOK_DEV
BF16 = jnp.bfloat16
F32 = jnp.float32
VMEM_LIMIT = 40 * 1024 * 1024


def from_behind(value, axis, steps):
    count = lax.axis_size(axis)
    pairs = [(source, (source + steps) % count) for source in range(count)]
    return lax.ppermute(value, axis, pairs)


def layer_norm(values):
    center = values - jnp.mean(values, axis=-1, keepdims=True)
    spread = jnp.mean(center * center, axis=-1, keepdims=True)
    return center * lax.rsqrt(spread + 1e-06)


def sigma_table():
    fraction = jnp.arange(LEVELS + 1).astype(jnp.float32) / LEVELS
    return 5.0 * fraction / (1.0 + 4.0 * fraction)


def norm_rope(values, gain_row, position):
    row_count = values.shape[0]
    floats = values.astype(jnp.float32)
    scaled = (
        floats * lax.rsqrt(jnp.mean(floats * floats, axis=-1, keepdims=True) + 1e-06) * gain_row
    )
    halves = HEAD_DIM // 2
    scaled = scaled.reshape(row_count, HEADS, HEAD_DIM)
    frequency = jnp.power(10000.0, -jnp.arange(halves).astype(jnp.float32) / halves)
    angles = position[:, None, None] * frequency[None, None, :]
    cosines = jnp.cos(angles)
    sines = jnp.sin(angles)
    front_half = scaled[..., :halves]
    back_half = scaled[..., halves:]
    turned = jnp.concatenate(
        [front_half * cosines - back_half * sines, front_half * sines + back_half * cosines],
        axis=-1,
    )
    return turned.reshape(row_count, ATT).astype(jnp.bfloat16)


def group_parts(queries, key_rows, value_rows):
    row_count = queries.shape[0]
    key_count = key_rows.shape[0]
    query_heads = queries.reshape(row_count, HEADS, HEAD_DIM).transpose(1, 0, 2)
    key_heads = key_rows.reshape(key_count, HEADS, HEAD_DIM).transpose(1, 0, 2)
    value_heads = value_rows.reshape(key_count, HEADS, HEAD_DIM).transpose(1, 0, 2)

    def one_head(operands):
        query_part, key_part, value_part = operands
        scores = jnp.einsum(
            "rd,kd->rk", query_part, key_part, preferred_element_type=jnp.float32
        ) * HEAD_DIM ** (-0.5)
        maxima = jnp.max(scores, axis=-1)
        weights = jnp.exp(scores - maxima[:, None]).astype(jnp.bfloat16)
        totals = jnp.sum(weights.astype(jnp.float32), axis=-1)
        output = jnp.dot(weights, value_part, preferred_element_type=jnp.float32)
        return (output, maxima, totals)

    output, maxima, totals = lax.map(one_head, (query_heads, key_heads, value_heads))
    return (output.transpose(1, 0, 2).reshape(row_count, ATT), maxima.T, totals.T)


def general(
    stream, latents, time_mod, block_mod, w_qkv, qk_gain, w_out, head_mod, w_head, noise_level
):
    slab_count = lax.axis_size("slab")
    seq_count = lax.axis_size("seq")
    slab_index = lax.axis_index("slab")
    seq_index = lax.axis_index("seq")
    group_rows = TOK_DEV * seq_count
    hidden = stream[0].astype(jnp.float32)
    modulation = block_mod + time_mod[0]
    modded = (layer_norm(hidden) * (1.0 + modulation[1]) + modulation[0]).astype(jnp.bfloat16)
    columns = jnp.dot(
        lax.all_gather(modded, "seq", axis=0, tiled=True), w_qkv, preferred_element_type=jnp.float32
    ).astype(jnp.bfloat16)
    own_position = (slab_index * group_rows + seq_index * TOK_DEV + jnp.arange(TOK_DEV)).astype(
        jnp.float32
    )
    full_mixed = lax.all_gather(columns, "seq", axis=1, tiled=True)
    own_mixed = lax.dynamic_slice_in_dim(full_mixed, seq_index * TOK_DEV, TOK_DEV, 0)
    own_queries = norm_rope(own_mixed[:, :ATT], qk_gain[0], own_position)
    group_position = (slab_index * group_rows + jnp.arange(group_rows)).astype(jnp.float32)
    group_keys = norm_rope(full_mixed[:, ATT : 2 * ATT], qk_gain[1], group_position)
    group_values = full_mixed[:, 2 * ATT :]
    all_queries = lax.all_gather(own_queries[None], "slab", axis=0, tiled=True)
    slab_ids = jnp.arange(slab_count)
    output, maxima, totals = group_parts(
        all_queries.reshape(slab_count * TOK_DEV, ATT), group_keys, group_values
    )
    usable = (slab_ids >= slab_index)[:, None, None]
    output = jnp.where(usable, output.reshape(slab_count, TOK_DEV, ATT), 0.0)
    maxima = jnp.where(usable, maxima.reshape(slab_count, TOK_DEV, HEADS), -1e30)
    totals = jnp.where(usable, totals.reshape(slab_count, TOK_DEV, HEADS), 0.0)
    recv_out, recv_max, recv_sum = (
        lax.all_to_all(output, "slab", split_axis=0, concat_axis=0, tiled=True),
        lax.all_to_all(maxima, "slab", split_axis=0, concat_axis=0, tiled=True),
        lax.all_to_all(totals, "slab", split_axis=0, concat_axis=0, tiled=True),
    )
    highest = jnp.max(recv_max, axis=0)
    weights = jnp.exp(recv_max - highest)
    total_sum = jnp.sum(recv_sum * weights, axis=0)
    accum = jnp.sum(
        recv_out.reshape(slab_count, TOK_DEV, HEADS, HEAD_DIM) * weights[..., None], axis=0
    )
    attended = (accum / total_sum[..., None]).reshape(TOK_DEV, ATT).astype(jnp.bfloat16)
    projected = jnp.dot(attended, w_out, preferred_element_type=jnp.float32)
    updated = hidden + modulation[2] * projected
    head_in = (layer_norm(updated) * (1.0 + head_mod[0, 1]) + head_mod[0, 0]).astype(jnp.bfloat16)
    velocity = jnp.dot(head_in, w_head, preferred_element_type=jnp.float32)
    table = sigma_table()
    level_ids = jnp.arange(LEVELS + 1)
    current_level = noise_level[0]
    sigma_now = jnp.sum(jnp.where(level_ids == current_level, table, 0.0))
    sigma_next = jnp.sum(jnp.where(level_ids == current_level - 1, table, 0.0))
    stepped = latents[0] + (sigma_next - sigma_now) * velocity
    moved = from_behind(stepped[None], "slab", -1)
    return (updated.astype(jnp.bfloat16)[None], moved)


def vmem_call(kernel, outs, name, flops, scratch=(), placed=0):
    whole = pl.BlockSpec(memory_space=pltpu.VMEM)
    stay = pl.BlockSpec(memory_space=pltpu.HBM)

    def call(*operands):
        return pl.pallas_call(
            kernel,
            out_shape=[jax.ShapeDtypeStruct(shape, dtype) for shape, dtype in outs],
            in_specs=[whole] * (len(operands) - placed) + [stay] * placed,
            out_specs=[whole] * len(outs),
            scratch_shapes=list(scratch),
            compiler_params=pltpu.CompilerParams(vmem_limit_bytes=VMEM_LIMIT),
            cost_estimate=pl.CostEstimate(flops=flops, bytes_accessed=1 << 20, transcendentals=0),
            name=name,
        )(*operands)

    return call


def here():
    slab, seq = lax.axis_index("slab"), lax.axis_index("seq")
    return seq // 2, seq % 2, slab % 2, slab // 2


def dot_rows(left, right):
    return lax.dot_general(left, right, (((1,), (1,)), ((), ())), preferred_element_type=F32)


def modulated(rows, time_mod, block_mod):
    shift = block_mod[0:1] + time_mod[0]
    scale = 1.0 + (block_mod[1:2] + time_mod[1])
    return (layer_norm(rows[...].astype(F32)) * scale + shift).astype(BF16)


def first_kernel(
    x2, x1, x3, x0, time_mod, block_mod, w_own, w_first, modded, own, other
):
    for place, rows in enumerate((x2, x1, x3, x0)):
        modded[place * TOK_DEV : (place + 1) * TOK_DEV, :] = modulated(rows, time_mod, block_mod)
    half = D // 2
    at = pl.multiple_of(here()[2] * half, half)
    own[...] = jnp.dot(modded[...], w_own[...], preferred_element_type=F32).astype(BF16)
    other[...] = jnp.dot(modded[:, pl.ds(at, half)], w_first[...], preferred_element_type=F32)


def project_kernel(
    w_second, modded, own_in, other_in, far_out, near_out, keep_out, sums_out, mixed
):
    line, side, core, _ = here()
    half = D // 2
    width = w_second.shape[1]
    at = pl.multiple_of((1 - core) * half, half)
    other = jnp.dot(modded[:, pl.ds(at, half)], w_second[...], preferred_element_type=F32)
    other = (other + other_in[...]).astype(BF16)
    mine = pl.multiple_of(side * width, width)
    there = pl.multiple_of((1 - side) * width, width)
    for place, step in enumerate((2, 1, 3, 0)):
        at = pl.multiple_of(jnp.bitwise_xor(line, step) * TOK_DEV, 16)
        rows = slice(place * TOK_DEV, (place + 1) * TOK_DEV)
        mixed[pl.ds(at, TOK_DEV), pl.ds(mine, width)] = own_in[rows, :]
        mixed[pl.ds(at, TOK_DEV), pl.ds(there, width)] = other[rows]
    ones = jnp.ones((16, PAIR), BF16)
    row_id = lax.broadcasted_iota(jnp.int32, (16, ROWS), 0)
    picked = jnp.zeros((16, ROWS), F32)
    for unit in range(3):
        values = mixed[:, unit * PAIR : (unit + 1) * PAIR].astype(F32)
        squares = values * values
        high = squares.astype(BF16)
        low = (squares - high.astype(F32)).astype(BF16)
        total = dot_rows(ones, high) + dot_rows(ones, low)
        kind = (line * 3 + unit) // LINE
        picked += jnp.where(row_id // 3 == kind, total, 0.0)
    picked = jnp.where(row_id < 6, picked, 0.0)
    first = picked.astype(BF16).astype(F32)
    second = (picked - first).astype(BF16).astype(F32)
    third = picked - first - second
    part = row_id % 3
    packed = jnp.where(part == 0, first, jnp.where(part == 1, second, third)).astype(BF16)
    padded = jnp.concatenate([packed, jnp.zeros((16, PAIR - ROWS), BF16)], axis=1)
    sums_out[...] = padded
    near_out[:ROWS, :] = mixed[:, PAIR : 2 * PAIR]
    near_out[ROWS:, :] = padded
    odd = line % 2
    at = pl.multiple_of((1 - odd) * 2 * PAIR, PAIR)
    far_out[:ROWS, :] = mixed[:, pl.ds(at, PAIR)]
    far_out[ROWS:, :] = padded
    at = pl.multiple_of(odd * 2 * PAIR, PAIR)
    keep_out[...] = mixed[:, pl.ds(at, PAIR)]


def step_size(levels):
    level = jnp.broadcast_to(levels[...], (1, HEAD_DIM))

    def sigma(level):
        fraction = level.astype(F32) / LEVELS
        return 5.0 * fraction / (1.0 + 4.0 * fraction)

    return sigma(level - 1) - sigma(level)


def rope_kernel(
    far, last_sums, near, keep, own_sums, gains, cosines, sines, levels, q_out, kv_out, size, units
):
    line, _, _, _ = here()
    upper, odd = line // 2, line % 2
    slots = (
        jnp.where(upper == 1, 2, odd),
        jnp.where((line == 0) | (line == 3), 1, 0),
        jnp.where(upper == 0, 2, 1 - odd),
    )
    units[0] = keep[...]
    units[1] = near[:ROWS, :]
    units[2] = far[:ROWS, :]
    pieces = [
        own_sums[...].astype(F32), near[ROWS:, :].astype(F32),
        far[ROWS:, :].astype(F32), last_sums[...].astype(F32),
    ]
    row_id = lax.broadcasted_iota(jnp.int32, (16, 1), 0)
    cos, sin = cosines[...], sines[...]
    for kind in range(2):
        wanted = row_id // 3 == kind
        total = jnp.zeros((1, PAIR), F32)
        for piece in pieces:
            total += jnp.sum(jnp.where(wanted, piece, 0.0), axis=0, keepdims=True)
        scale = lax.rsqrt(total * (1.0 / ATT) + 1e-06)
        scale = jnp.transpose(jnp.broadcast_to(scale, (HEAD_DIM, PAIR)))[:ROWS]
        values = units[slots[kind]].astype(F32)
        for head in range(2):
            columns = slice(head * HEAD_DIM, (head + 1) * HEAD_DIM)
            at = pl.multiple_of(line * PAIR + head * HEAD_DIM, HEAD_DIM)
            scaled = values[:, columns] * scale * gains[kind : kind + 1, pl.ds(at, HEAD_DIM)]
            turned = scaled * cos + pltpu.roll(scaled, HEAD_DIM // 2, axis=1) * sin
            (kv_out if kind else q_out)[:, columns] = turned.astype(BF16)
    kv_out[:, PAIR:] = units[slots[2]]
    size[...] = step_size(levels)


def attend_group(queries, one, two, head, counts=None):
    columns = slice(head * HEAD_DIM, (head + 1) * HEAD_DIM)
    value_columns = slice(PAIR + head * HEAD_DIM, PAIR + (head + 1) * HEAD_DIM)
    keys = jnp.concatenate([one[:, columns], two[:, columns]], axis=0)
    values = jnp.concatenate([one[:, value_columns], two[:, value_columns]], axis=0)
    ones = jnp.ones((2 * ROWS, HEAD_DIM), BF16)
    scores = dot_rows(queries[:, columns], keys) * HEAD_DIM ** (-0.5)
    maxima = jnp.max(scores, axis=-1, keepdims=True)
    weights = jnp.exp(scores - maxima).astype(BF16)
    output = jnp.dot(weights, jnp.concatenate([values, ones], axis=1), preferred_element_type=F32)
    if counts is not None:
        maxima = jnp.where(counts, maxima, -1e30)
    return output, maxima


def merged(parts):
    highest = functools.reduce(jnp.maximum, [maxima for _, maxima in parts])
    total = sum(output * jnp.exp(maxima - highest) for output, maxima in parts)
    return total, highest


def first_attend_kernel(queries, c0, c1, a0, a1, total_out, highest_out):
    chip = here()[3]
    for head in range(2):
        own = attend_group(queries, a0, a1, head)
        far = attend_group(queries, c0, c1, head, chip == 1)
        total, highest = merged([own, far])
        total_out[head] = total
        highest_out[head] = jnp.broadcast_to(highest, (ROWS, HEAD_DIM))


def last_attend_kernel(
    queries, b0, b1, d0, d1, total_in, highest_in, o3, o2, o1, o0, result
):
    line, _, core, chip = here()
    for head in range(2):
        near = attend_group(queries, b0, b1, head, core == 1)
        far = attend_group(queries, d0, d1, head, chip == 1)
        total, _ = merged([(total_in[head], highest_in[head, :, :1]), near, far])
        columns = slice(head * HEAD_DIM, (head + 1) * HEAD_DIM)
        result[:, columns] = (total[:, :HEAD_DIM] / total[:, HEAD_DIM:]).astype(BF16)
    for step, out in enumerate((o0, o1, o2, o3)):
        at = pl.multiple_of(jnp.bitwise_xor(line, step) * TOK_DEV, 16)
        out[...] = result[pl.ds(at, TOK_DEV), :]


def load(sources, held, arrived):
    copies = [
        pltpu.make_async_copy(source, target, arrived.at[i])
        for i, (source, target) in enumerate(zip(sources, held))
    ]
    for copy in copies:
        copy.start()
    return copies


def times_w_out(rows, w_out, step):
    at = pl.multiple_of(jnp.bitwise_xor(here()[0], step) * PAIR, PAIR)
    return jnp.dot(rows[...], w_out[pl.ds(at, PAIR), :], preferred_element_type=F32)


def begin_kernel(
    r0, w_out, stream_in, time_in, block_in, head_in, base, vectors,
    stream, time_mod, block_mod, head_mod, arrived,
):
    copies = load(
        (stream_in, time_in, block_in, head_in), (stream, time_mod, block_mod, head_mod), arrived
    )
    projected = times_w_out(r0, w_out, 0)
    for copy in copies:
        copy.wait()
    gate = block_mod[2:3] + time_mod[2]
    base[...] = stream[...].astype(F32) + gate * projected
    vectors[0:1] = gate
    vectors[1:2] = 1.0 + head_mod[1:2]
    vectors[2:3] = head_mod[0:1]


def finish_kernel(
    r3, r2, r1, w_out, base, vectors, w_head, size, latents_in, stream_out, latents_out,
    latents, arrived,
):
    copies = load((latents_in,), (latents,), arrived)
    projected = times_w_out(r3, w_out, 3) + times_w_out(r2, w_out, 2) + times_w_out(r1, w_out, 1)
    updated = base[...] + vectors[0:1] * projected
    stream_out[...] = updated
    head_in = (layer_norm(updated) * vectors[1:2] + vectors[2:3]).astype(BF16)
    velocity = dot_rows(head_in, w_head[...])

    copies[0].wait()
    latents_out[...] = latents[...] + size[0:1, :CHAN] * velocity


def lines(
    stream, latents, time_mod, block_mod, w_qkv, qk_gain, w_out, head_mod, w_head, noise_level
):
    slab, seq = lax.axis_index("slab"), lax.axis_index("seq")
    side, core = seq % 2, slab % 2

    def along(step, value):
        return lax.ppermute(value, "seq", [(i, i ^ (2 * step)) for i in range(2 * LINE)])

    def across(value):
        return lax.ppermute(value, "seq", [(i, i ^ 1) for i in range(2 * LINE)])

    def cores(value):
        return lax.ppermute(value, "slab", [(i, i ^ 1) for i in range(4)])

    def chips(value):
        return lax.ppermute(value, "slab", [(i, i ^ 2) for i in range(4)])

    def chips_and_sides(value):
        count = 2 * LINE
        pairs = [
            (s * count + i, (s ^ 2) * count + (i ^ 1 if s < 2 else i))
            for s in range(4)
            for i in range(count)
        ]
        return lax.ppermute(value, ("slab", "seq"), pairs)

    rows = stream[0]
    time_rows = time_mod.transpose(1, 0, 2)
    w_first = across(lax.dynamic_slice_in_dim(w_qkv, core * (D // 2), D // 2, 0))
    x3, x2, x1 = along(3, rows), along(2, rows), along(1, rows)
    at = (jnp.arange(LINE)[:, None] * 2 + side) * TOK_DEV + jnp.arange(TOK_DEV)[None]
    position = (slab * (2 * LINE * TOK_DEV) + at.reshape(ROWS)).astype(F32)
    halves = HEAD_DIM // 2
    frequency = jnp.power(10000.0, -jnp.arange(halves).astype(F32) / halves)
    angles = position[:, None] * frequency[None]
    cosines, sines = jnp.cos(angles), jnp.sin(angles)
    cosines = jnp.concatenate([cosines, cosines], axis=1)
    sines = jnp.concatenate([-sines, sines], axis=1)

    w_second = cores(w_first)
    width = w_qkv.shape[1]
    modded, own, other = vmem_call(
        first_kernel, [((ROWS, D), BF16), ((ROWS, width), BF16), ((ROWS, width), F32)],
        "first", 1 << 28,
    )(x2, x1, x3, rows, time_rows, block_mod, w_qkv, w_first)
    message = (ROWS + 16, PAIR)
    far, near, keep, sums = vmem_call(
        project_kernel,
        [(message, BF16), (message, BF16), ((ROWS, PAIR), BF16), ((16, PAIR), BF16)],
        "project", 1 << 28, [pltpu.VMEM((ROWS, 3 * PAIR), BF16)],
    )(w_second, modded, own, other)
    far, last_sums, near = along(2, far), along(3, sums), along(1, near)
    queries, pairs, size = vmem_call(
        rope_kernel,
        [((ROWS, PAIR), BF16), ((ROWS, 2 * PAIR), BF16), ((1, HEAD_DIM), F32)],
        "rope", 1 << 22, [pltpu.VMEM((3, ROWS, PAIR), BF16)],
    )(far, last_sums, near, keep, sums, qk_gain, cosines, sines, noise_level[None])
    chip_pairs, side_pairs = chips(pairs), across(pairs)
    both_pairs = chips_and_sides(pairs)
    chip_pairs, side_pairs = lax.optimization_barrier((chip_pairs, side_pairs))
    state = [((2, ROWS, PAIR), F32), ((2, ROWS, HEAD_DIM), F32)]
    now = vmem_call(first_attend_kernel, state, "attend_first", 1 << 27)(
        queries, chip_pairs, both_pairs, pairs, side_pairs
    )
    _, late_pairs = lax.optimization_barrier((side_pairs, pairs))
    core_pairs = cores(late_pairs)
    core_side, core_chip, core_both = cores(side_pairs), cores(chip_pairs), cores(both_pairs)
    part3, part2, part1, part0 = vmem_call(
        last_attend_kernel, [((TOK_DEV, PAIR), BF16)] * 4, "attend_last", 1 << 27,
        [pltpu.VMEM((ROWS, PAIR), BF16)],
    )(queries, core_pairs, core_side, core_chip, core_both, *now)
    late = [along(3, part3), along(2, part2), along(1, part1)]
    loaded = (rows, time_rows, block_mod, head_mod[0])
    base, vectors = vmem_call(
        begin_kernel, [((TOK_DEV, D), F32), ((8, D), F32)], "begin", 1 << 28,
        [pltpu.VMEM(v.shape, v.dtype) for v in loaded] + [pltpu.SemaphoreType.DMA((len(loaded),))],
        placed=len(loaded),
    )(part0, w_out, *loaded)
    updated, stepped = vmem_call(
        finish_kernel, [((TOK_DEV, D), F32), ((TOK_DEV, CHAN), F32)], "finish", 1 << 28,
        [pltpu.VMEM((TOK_DEV, CHAN), F32), pltpu.SemaphoreType.DMA((1,))], placed=1,
    )(*late, w_out, base, vectors, w_head.T, size, latents[0])
    return (updated.astype(BF16)[None], from_behind(stepped[None], "slab", -1))


def solution(mesh):
    in_specs = (
        P("slab", "seq", None),
        P("slab", "seq", None),
        P("slab", None, None),
        P(),
        P(None, "seq"),
        P(),
        P(),
        P("slab", None, None),
        P(),
        P("slab"),
    )
    out_specs = (P("slab", "seq", None), P("slab", "seq", None))
    local = lines if tuple(mesh.shape.values()) == (4, 2 * LINE) else general
    return jax.shard_map(local, mesh=mesh, in_specs=in_specs, out_specs=out_specs, check_vma=False)
```

```python
import functools

import jax
import jax.numpy as jnp
from jax import lax
from jax.experimental import pallas as pl
from jax.experimental.pallas import tpu as pltpu
from jax.sharding import PartitionSpec as P

HEADS = 8
HEAD_DIM = 128
LEVELS = 32
TOK_DEV = 48
ATT = 1024
D = 1536
CHAN = 64
PAIR = 2 * HEAD_DIM
LINE = 4
ROWS = LINE * TOK_DEV
BF16 = jnp.bfloat16
F32 = jnp.float32
VMEM_LIMIT = 40 * 1024 * 1024


def from_behind(value, axis, steps):
    count = lax.axis_size(axis)
    pairs = [(source, (source + steps) % count) for source in range(count)]
    return lax.ppermute(value, axis, pairs)


def layer_norm(values):
    center = values - jnp.mean(values, axis=-1, keepdims=True)
    spread = jnp.mean(center * center, axis=-1, keepdims=True)
    return center * lax.rsqrt(spread + 1e-06)


def sigma_table():
    fraction = jnp.arange(LEVELS + 1).astype(jnp.float32) / LEVELS
    return 5.0 * fraction / (1.0 + 4.0 * fraction)


def norm_rope(values, gain_row, position):
    row_count = values.shape[0]
    floats = values.astype(jnp.float32)
    scaled = (
        floats * lax.rsqrt(jnp.mean(floats * floats, axis=-1, keepdims=True) + 1e-06) * gain_row
    )
    halves = HEAD_DIM // 2
    scaled = scaled.reshape(row_count, HEADS, HEAD_DIM)
    frequency = jnp.power(10000.0, -jnp.arange(halves).astype(jnp.float32) / halves)
    angles = position[:, None, None] * frequency[None, None, :]
    cosines = jnp.cos(angles)
    sines = jnp.sin(angles)
    front_half = scaled[..., :halves]
    back_half = scaled[..., halves:]
    turned = jnp.concatenate(
        [front_half * cosines - back_half * sines, front_half * sines + back_half * cosines],
        axis=-1,
    )
    return turned.reshape(row_count, ATT).astype(jnp.bfloat16)


def group_parts(queries, key_rows, value_rows):
    row_count = queries.shape[0]
    key_count = key_rows.shape[0]
    query_heads = queries.reshape(row_count, HEADS, HEAD_DIM).transpose(1, 0, 2)
    key_heads = key_rows.reshape(key_count, HEADS, HEAD_DIM).transpose(1, 0, 2)
    value_heads = value_rows.reshape(key_count, HEADS, HEAD_DIM).transpose(1, 0, 2)

    def one_head(operands):
        query_part, key_part, value_part = operands
        scores = jnp.einsum(
            "rd,kd->rk", query_part, key_part, preferred_element_type=jnp.float32
        ) * HEAD_DIM ** (-0.5)
        maxima = jnp.max(scores, axis=-1)
        weights = jnp.exp(scores - maxima[:, None]).astype(jnp.bfloat16)
        totals = jnp.sum(weights.astype(jnp.float32), axis=-1)
        output = jnp.dot(weights, value_part, preferred_element_type=jnp.float32)
        return (output, maxima, totals)

    output, maxima, totals = lax.map(one_head, (query_heads, key_heads, value_heads))
    return (output.transpose(1, 0, 2).reshape(row_count, ATT), maxima.T, totals.T)


def general(
    stream, latents, time_mod, block_mod, w_qkv, qk_gain, w_out, head_mod, w_head, noise_level
):
    slab_count = lax.axis_size("slab")
    seq_count = lax.axis_size("seq")
    slab_index = lax.axis_index("slab")
    seq_index = lax.axis_index("seq")
    group_rows = TOK_DEV * seq_count
    hidden = stream[0].astype(jnp.float32)
    modulation = block_mod + time_mod[0]
    modded = (layer_norm(hidden) * (1.0 + modulation[1]) + modulation[0]).astype(jnp.bfloat16)
    columns = jnp.dot(
        lax.all_gather(modded, "seq", axis=0, tiled=True), w_qkv, preferred_element_type=jnp.float32
    ).astype(jnp.bfloat16)
    own_position = (slab_index * group_rows + seq_index * TOK_DEV + jnp.arange(TOK_DEV)).astype(
        jnp.float32
    )
    full_mixed = lax.all_gather(columns, "seq", axis=1, tiled=True)
    own_mixed = lax.dynamic_slice_in_dim(full_mixed, seq_index * TOK_DEV, TOK_DEV, 0)
    own_queries = norm_rope(own_mixed[:, :ATT], qk_gain[0], own_position)
    group_position = (slab_index * group_rows + jnp.arange(group_rows)).astype(jnp.float32)
    group_keys = norm_rope(full_mixed[:, ATT : 2 * ATT], qk_gain[1], group_position)
    group_values = full_mixed[:, 2 * ATT :]
    all_queries = lax.all_gather(own_queries[None], "slab", axis=0, tiled=True)
    slab_ids = jnp.arange(slab_count)
    output, maxima, totals = group_parts(
        all_queries.reshape(slab_count * TOK_DEV, ATT), group_keys, group_values
    )
    usable = (slab_ids >= slab_index)[:, None, None]
    output = jnp.where(usable, output.reshape(slab_count, TOK_DEV, ATT), 0.0)
    maxima = jnp.where(usable, maxima.reshape(slab_count, TOK_DEV, HEADS), -1e30)
    totals = jnp.where(usable, totals.reshape(slab_count, TOK_DEV, HEADS), 0.0)
    recv_out, recv_max, recv_sum = (
        lax.all_to_all(output, "slab", split_axis=0, concat_axis=0, tiled=True),
        lax.all_to_all(maxima, "slab", split_axis=0, concat_axis=0, tiled=True),
        lax.all_to_all(totals, "slab", split_axis=0, concat_axis=0, tiled=True),
    )
    highest = jnp.max(recv_max, axis=0)
    weights = jnp.exp(recv_max - highest)
    total_sum = jnp.sum(recv_sum * weights, axis=0)
    accum = jnp.sum(
        recv_out.reshape(slab_count, TOK_DEV, HEADS, HEAD_DIM) * weights[..., None], axis=0
    )
    attended = (accum / total_sum[..., None]).reshape(TOK_DEV, ATT).astype(jnp.bfloat16)
    projected = jnp.dot(attended, w_out, preferred_element_type=jnp.float32)
    updated = hidden + modulation[2] * projected
    head_in = (layer_norm(updated) * (1.0 + head_mod[0, 1]) + head_mod[0, 0]).astype(jnp.bfloat16)
    velocity = jnp.dot(head_in, w_head, preferred_element_type=jnp.float32)
    table = sigma_table()
    level_ids = jnp.arange(LEVELS + 1)
    current_level = noise_level[0]
    sigma_now = jnp.sum(jnp.where(level_ids == current_level, table, 0.0))
    sigma_next = jnp.sum(jnp.where(level_ids == current_level - 1, table, 0.0))
    stepped = latents[0] + (sigma_next - sigma_now) * velocity
    moved = from_behind(stepped[None], "slab", -1)
    return (updated.astype(jnp.bfloat16)[None], moved)


def vmem_call(kernel, outs, name, flops, scratch=(), placed=0):
    whole = pl.BlockSpec(memory_space=pltpu.VMEM)
    stay = pl.BlockSpec(memory_space=pltpu.HBM)

    def call(*operands):
        return pl.pallas_call(
            kernel,
            out_shape=[jax.ShapeDtypeStruct(shape, dtype) for shape, dtype in outs],
            in_specs=[whole] * (len(operands) - placed) + [stay] * placed,
            out_specs=[whole] * len(outs),
            scratch_shapes=list(scratch),
            compiler_params=pltpu.CompilerParams(vmem_limit_bytes=VMEM_LIMIT),
            cost_estimate=pl.CostEstimate(flops=flops, bytes_accessed=1 << 20, transcendentals=0),
            name=name,
        )(*operands)

    return call


def here():
    slab, seq = lax.axis_index("slab"), lax.axis_index("seq")
    return seq // 2, seq % 2, slab % 2, slab // 2


def dot_rows(left, right):
    return lax.dot_general(left, right, (((1,), (1,)), ((), ())), preferred_element_type=F32)


def modulated(rows, shift_scale):
    return (layer_norm(rows[...].astype(F32)) * shift_scale[1:2] + shift_scale[0:1]).astype(BF16)


def prepare_kernel(x0, time_mod, block_mod, modded, shift_scale):
    shift_scale[0:1] = block_mod[0:1] + time_mod[0]
    shift_scale[1:2] = 1.0 + (block_mod[1:2] + time_mod[1])
    modded[...] = modulated(x0, shift_scale)


def first_kernel(
    x1, x2, x3, modded_own, shift_scale, w_own, w_mine, w_last, w_chip, modded, own, other
):
    for place, rows in enumerate((x2, x1, x3)):
        modded[place * TOK_DEV : (place + 1) * TOK_DEV, :] = modulated(rows, shift_scale)
    modded[3 * TOK_DEV :, :] = modded_own[...]
    _, _, core, chip = here()
    own[...] = jnp.dot(modded[...], w_own[...], preferred_element_type=F32).astype(BF16)
    total = part_product(modded, w_mine, 2 * chip + core)
    total += part_product(modded, w_last, 4 + core)
    other[...] = total + part_product(modded, w_chip, 2 * (1 - chip) + core)


def part_product(modded, weights, part):
    depth = weights.shape[0]
    at = pl.multiple_of(part * depth, depth)
    return jnp.dot(modded[:, pl.ds(at, depth)], weights[...], preferred_element_type=F32)


def project_kernel(
    w_core, w_core_last, w_core_chip, modded, own_in, other_in,
    far_out, near_out, keep_out, sums_out, mixed,
):
    line, side, core, chip = here()
    width = w_core.shape[1]
    total = other_in[...] + part_product(modded, w_core, 2 * chip + 1 - core)
    total += part_product(modded, w_core_last, 4 + 1 - core)
    total += part_product(modded, w_core_chip, 2 * (1 - chip) + 1 - core)
    other = total.astype(BF16)
    mine = pl.multiple_of(side * width, width)
    there = pl.multiple_of((1 - side) * width, width)
    for place, step in enumerate((2, 1, 3, 0)):
        at = pl.multiple_of(jnp.bitwise_xor(line, step) * TOK_DEV, 16)
        rows = slice(place * TOK_DEV, (place + 1) * TOK_DEV)
        mixed[pl.ds(at, TOK_DEV), pl.ds(mine, width)] = own_in[rows, :]
        mixed[pl.ds(at, TOK_DEV), pl.ds(there, width)] = other[rows]
    ones = jnp.ones((16, PAIR), BF16)
    row_id = lax.broadcasted_iota(jnp.int32, (16, ROWS), 0)
    picked = jnp.zeros((16, ROWS), F32)
    for unit in range(3):
        values = mixed[:, unit * PAIR : (unit + 1) * PAIR].astype(F32)
        squares = values * values
        high = squares.astype(BF16)
        low = (squares - high.astype(F32)).astype(BF16)
        total = dot_rows(ones, high) + dot_rows(ones, low)
        kind = (line * 3 + unit) // LINE
        picked += jnp.where(row_id // 3 == kind, total, 0.0)
    picked = jnp.where(row_id < 6, picked, 0.0)
    first = picked.astype(BF16).astype(F32)
    second = (picked - first).astype(BF16).astype(F32)
    third = picked - first - second
    part = row_id % 3
    packed = jnp.where(part == 0, first, jnp.where(part == 1, second, third)).astype(BF16)
    padded = jnp.concatenate([packed, jnp.zeros((16, PAIR - ROWS), BF16)], axis=1)
    sums_out[...] = padded
    near_out[:ROWS, :] = mixed[:, PAIR : 2 * PAIR]
    near_out[ROWS:, :] = padded
    odd = line % 2
    at = pl.multiple_of((1 - odd) * 2 * PAIR, PAIR)
    far_out[:ROWS, :] = mixed[:, pl.ds(at, PAIR)]
    far_out[ROWS:, :] = padded
    at = pl.multiple_of(odd * 2 * PAIR, PAIR)
    keep_out[...] = mixed[:, pl.ds(at, PAIR)]


def step_size(levels):
    level = jnp.broadcast_to(levels[...], (1, HEAD_DIM))

    def sigma(level):
        fraction = level.astype(F32) / LEVELS
        return 5.0 * fraction / (1.0 + 4.0 * fraction)

    return sigma(level - 1) - sigma(level)


def rope_kernel(
    near, far, last_sums, keep, own_sums, gains, cosines, sines, levels, q_out, kv_out, size, units
):
    line, _, _, _ = here()
    upper, odd = line // 2, line % 2
    slots = (
        jnp.where(upper == 1, 2, odd),
        jnp.where((line == 0) | (line == 3), 1, 0),
        jnp.where(upper == 0, 2, 1 - odd),
    )
    units[0] = keep[...]
    units[1] = near[:ROWS, :]
    units[2] = far[:ROWS, :]
    pieces = [
        own_sums[...].astype(F32), near[ROWS:, :].astype(F32),
        far[ROWS:, :].astype(F32), last_sums[...].astype(F32),
    ]
    row_id = lax.broadcasted_iota(jnp.int32, (16, 1), 0)
    cos, sin = cosines[...], sines[...]
    for kind in range(2):
        wanted = row_id // 3 == kind
        total = jnp.zeros((1, PAIR), F32)
        for piece in pieces:
            total += jnp.sum(jnp.where(wanted, piece, 0.0), axis=0, keepdims=True)
        scale = lax.rsqrt(total * (1.0 / ATT) + 1e-06)
        scale = jnp.transpose(jnp.broadcast_to(scale, (HEAD_DIM, PAIR)))[:ROWS]
        values = units[slots[kind]].astype(F32)
        for head in range(2):
            columns = slice(head * HEAD_DIM, (head + 1) * HEAD_DIM)
            at = pl.multiple_of(line * PAIR + head * HEAD_DIM, HEAD_DIM)
            scaled = values[:, columns] * scale * gains[kind : kind + 1, pl.ds(at, HEAD_DIM)]
            turned = scaled * cos + pltpu.roll(scaled, HEAD_DIM // 2, axis=1) * sin
            (kv_out if kind else q_out)[:, columns] = turned.astype(BF16)
    kv_out[:, PAIR:] = units[slots[2]]
    size[...] = step_size(levels)


def attend_group(queries, one, two, head, counts=None):
    columns = slice(head * HEAD_DIM, (head + 1) * HEAD_DIM)
    value_columns = slice(PAIR + head * HEAD_DIM, PAIR + (head + 1) * HEAD_DIM)
    keys = jnp.concatenate([one[:, columns], two[:, columns]], axis=0)
    values = jnp.concatenate([one[:, value_columns], two[:, value_columns]], axis=0)
    ones = jnp.ones((2 * ROWS, HEAD_DIM), BF16)
    scores = dot_rows(queries[:, columns], keys) * HEAD_DIM ** (-0.5)
    maxima = jnp.max(scores, axis=-1, keepdims=True)
    weights = jnp.exp(scores - maxima).astype(BF16)
    output = jnp.dot(weights, jnp.concatenate([values, ones], axis=1), preferred_element_type=F32)
    if counts is not None:
        maxima = jnp.where(counts, maxima, -1e30)
    return output, maxima


def merged(parts):
    highest = functools.reduce(jnp.maximum, [maxima for _, maxima in parts])
    total = sum(output * jnp.exp(maxima - highest) for output, maxima in parts)
    return total, highest


def first_attend_kernel(queries, c0, c1, a0, a1, total_out, highest_out):
    chip = here()[3]
    for head in range(2):
        own = attend_group(queries, a0, a1, head)
        far = attend_group(queries, c0, c1, head, chip == 1)
        total, highest = merged([own, far])
        total_out[head] = total
        highest_out[head] = jnp.broadcast_to(highest, (ROWS, HEAD_DIM))


def last_attend_kernel(
    queries, b0, b1, d0, d1, total_in, highest_in, o3, o2, o1, o0, result
):
    line, _, core, chip = here()
    for head in range(2):
        near = attend_group(queries, b0, b1, head, core == 1)
        far = attend_group(queries, d0, d1, head, chip == 1)
        total, _ = merged([(total_in[head], highest_in[head, :, :1]), near, far])
        columns = slice(head * HEAD_DIM, (head + 1) * HEAD_DIM)
        result[:, columns] = (total[:, :HEAD_DIM] / total[:, HEAD_DIM:]).astype(BF16)
    for step, out in enumerate((o0, o1, o2, o3)):
        at = pl.multiple_of(jnp.bitwise_xor(line, step) * TOK_DEV, 16)
        out[...] = result[pl.ds(at, TOK_DEV), :]


def load(sources, held, arrived):
    copies = [
        pltpu.make_async_copy(source, target, arrived.at[i])
        for i, (source, target) in enumerate(zip(sources, held))
    ]
    for copy in copies:
        copy.start()
    return copies


def times_w_out(rows, w_out, step):
    at = pl.multiple_of(jnp.bitwise_xor(here()[0], step) * PAIR, PAIR)
    return jnp.dot(rows[...], w_out[pl.ds(at, PAIR), :], preferred_element_type=F32)


def begin_kernel(
    r0, w_out, stream_in, time_in, block_in, head_in, base, vectors,
    stream, time_mod, block_mod, head_mod, arrived,
):
    copies = load(
        (stream_in, time_in, block_in, head_in), (stream, time_mod, block_mod, head_mod), arrived
    )
    projected = times_w_out(r0, w_out, 0)
    for copy in copies:
        copy.wait()
    gate = block_mod[2:3] + time_mod[2]
    base[...] = stream[...].astype(F32) + gate * projected
    vectors[0:1] = gate
    vectors[1:2] = 1.0 + head_mod[1:2]
    vectors[2:3] = head_mod[0:1]


def finish_kernel(
    r3, r2, r1, w_out, base, vectors, w_head, size, latents_in, stream_out, latents_out,
    latents, arrived,
):
    copies = load((latents_in,), (latents,), arrived)
    projected = times_w_out(r3, w_out, 3) + times_w_out(r2, w_out, 2) + times_w_out(r1, w_out, 1)
    updated = base[...] + vectors[0:1] * projected
    stream_out[...] = updated
    head_in = (layer_norm(updated) * vectors[1:2] + vectors[2:3]).astype(BF16)
    velocity = dot_rows(head_in, w_head[...])

    copies[0].wait()
    latents_out[...] = latents[...] + size[0:1, :CHAN] * velocity


def lines(
    stream, latents, time_mod, block_mod, w_qkv, qk_gain, w_out, head_mod, w_head, noise_level
):
    slab, seq = lax.axis_index("slab"), lax.axis_index("seq")
    side, core = seq % 2, slab % 2

    def along(step, value):
        return lax.ppermute(value, "seq", [(i, i ^ (2 * step)) for i in range(2 * LINE)])

    def across(value):
        return lax.ppermute(value, "seq", [(i, i ^ 1) for i in range(2 * LINE)])

    def cores(value):
        return lax.ppermute(value, "slab", [(i, i ^ 1) for i in range(4)])

    def chips(value):
        return lax.ppermute(value, "slab", [(i, i ^ 2) for i in range(4)])

    def chips_and_sides(value):
        count = 2 * LINE
        pairs = [
            (s * count + i, (s ^ 2) * count + (i ^ 1 if s < 2 else i))
            for s in range(4)
            for i in range(count)
        ]
        return lax.ppermute(value, ("slab", "seq"), pairs)

    rows = stream[0]
    time_rows = time_mod.transpose(1, 0, 2)
    depth = D // 6
    half_mine = lax.dynamic_slice_in_dim(w_qkv, (slab // 2 * 2 + core) * depth, depth, 0)
    half_last = lax.dynamic_slice_in_dim(w_qkv, (4 + core) * depth, depth, 0)
    w_mine, w_last = across(half_mine), across(half_last)
    late_rows, _ = lax.optimization_barrier((rows, half_mine))
    x1, x2, x3 = along(1, rows), along(2, rows), along(3, rows)

    at = (jnp.arange(LINE)[:, None] * 2 + side) * TOK_DEV + jnp.arange(TOK_DEV)[None]
    position = (slab * (2 * LINE * TOK_DEV) + at.reshape(ROWS)).astype(F32)
    halves = HEAD_DIM // 2
    frequency = jnp.power(10000.0, -jnp.arange(halves).astype(F32) / halves)
    angles = position[:, None] * frequency[None]
    cosines, sines = jnp.cos(angles), jnp.sin(angles)
    cosines = jnp.concatenate([cosines, cosines], axis=1)
    sines = jnp.concatenate([-sines, sines], axis=1)
    modded_own, shift_scale = vmem_call(
        prepare_kernel, [((TOK_DEV, D), BF16), ((2, D), F32)], "prepare", 1 << 20
    )(rows, time_rows, block_mod)
    w_chip = chips(w_mine)
    w_last, modded_own, shift_scale = lax.optimization_barrier((w_last, modded_own, shift_scale))
    w_core_last = cores(w_last)
    w_mine, w_chip = lax.optimization_barrier((w_mine, w_chip))
    w_core, w_core_chip = cores(w_mine), cores(w_chip)
    width = w_qkv.shape[1]
    modded, own, other = vmem_call(
        first_kernel, [((ROWS, D), BF16), ((ROWS, width), BF16), ((ROWS, width), F32)],
        "first", 1 << 28,
    )(x1, x2, x3, modded_own, shift_scale, w_qkv, w_mine, w_last, w_chip)
    message = (ROWS + 16, PAIR)
    far, near, keep, sums = vmem_call(
        project_kernel,
        [(message, BF16), (message, BF16), ((ROWS, PAIR), BF16), ((16, PAIR), BF16)],
        "project", 1 << 28, [pltpu.VMEM((ROWS, 3 * PAIR), BF16)],
    )(w_core, w_core_last, w_core_chip, modded, own, other)
    far, last_sums, near = along(2, far), along(3, sums), along(1, near)
    queries, pairs, size = vmem_call(
        rope_kernel,
        [((ROWS, PAIR), BF16), ((ROWS, 2 * PAIR), BF16), ((1, HEAD_DIM), F32)],
        "rope", 1 << 22, [pltpu.VMEM((3, ROWS, PAIR), BF16)],
    )(near, far, last_sums, keep, sums, qk_gain, cosines, sines, noise_level[None])
    chip_pairs, side_pairs = chips(pairs), across(pairs)
    both_pairs = chips_and_sides(pairs)
    chip_pairs, side_pairs = lax.optimization_barrier((chip_pairs, side_pairs))
    state = [((2, ROWS, PAIR), F32), ((2, ROWS, HEAD_DIM), F32)]
    now = vmem_call(first_attend_kernel, state, "attend_first", 1 << 27)(
        queries, chip_pairs, both_pairs, pairs, side_pairs
    )
    _, late_pairs = lax.optimization_barrier((side_pairs, pairs))
    core_pairs = cores(late_pairs)
    core_side, core_chip, core_both = cores(side_pairs), cores(chip_pairs), cores(both_pairs)
    part3, part2, part1, part0 = vmem_call(
        last_attend_kernel, [((TOK_DEV, PAIR), BF16)] * 4, "attend_last", 1 << 27,
        [pltpu.VMEM((ROWS, PAIR), BF16)],
    )(queries, core_pairs, core_side, core_chip, core_both, *now)
    late = [along(3, part3), along(2, part2), along(1, part1)]
    loaded = (rows, time_rows, block_mod, head_mod[0])
    base, vectors = vmem_call(
        begin_kernel, [((TOK_DEV, D), F32), ((8, D), F32)], "begin", 1 << 28,
        [pltpu.VMEM(v.shape, v.dtype) for v in loaded] + [pltpu.SemaphoreType.DMA((len(loaded),))],
        placed=len(loaded),
    )(part0, w_out, *loaded)
    updated, stepped = vmem_call(
        finish_kernel, [((TOK_DEV, D), F32), ((TOK_DEV, CHAN), F32)], "finish", 1 << 28,
        [pltpu.VMEM((TOK_DEV, CHAN), F32), pltpu.SemaphoreType.DMA((1,))], placed=1,
    )(*late, w_out, base, vectors, w_head.T, size, latents[0])
    return (updated.astype(BF16)[None], from_behind(stepped[None], "slab", -1))


def solution(mesh):
    in_specs = (
        P("slab", "seq", None),
        P("slab", "seq", None),
        P("slab", None, None),
        P(),
        P(None, "seq"),
        P(),
        P(),
        P("slab", None, None),
        P(),
        P("slab"),
    )
    out_specs = (P("slab", "seq", None), P("slab", "seq", None))
    local = lines if tuple(mesh.shape.values()) == (4, 2 * LINE) else general
    return jax.shard_map(local, mesh=mesh, in_specs=in_specs, out_specs=out_specs, check_vma=False)
```

```python
import functools

import jax
import jax.numpy as jnp
from jax import lax
from jax.experimental import pallas as pl
from jax.experimental.pallas import tpu as pltpu
from jax.sharding import PartitionSpec as P

HEADS = 8
HEAD_DIM = 128
LEVELS = 32
TOK_DEV = 48
ATT = 1024
D = 1536
CHAN = 64
PAIR = 2 * HEAD_DIM
LINE = 4
ROWS = LINE * TOK_DEV
BF16 = jnp.bfloat16
F32 = jnp.float32
VMEM_LIMIT = 40 * 1024 * 1024


def from_behind(value, axis, steps):
    count = lax.axis_size(axis)
    pairs = [(source, (source + steps) % count) for source in range(count)]
    return lax.ppermute(value, axis, pairs)


def layer_norm(values):
    center = values - jnp.mean(values, axis=-1, keepdims=True)
    spread = jnp.mean(center * center, axis=-1, keepdims=True)
    return center * lax.rsqrt(spread + 1e-06)


def sigma_table():
    fraction = jnp.arange(LEVELS + 1).astype(jnp.float32) / LEVELS
    return 5.0 * fraction / (1.0 + 4.0 * fraction)


def norm_rope(values, gain_row, position):
    row_count = values.shape[0]
    floats = values.astype(jnp.float32)
    scaled = (
        floats * lax.rsqrt(jnp.mean(floats * floats, axis=-1, keepdims=True) + 1e-06) * gain_row
    )
    halves = HEAD_DIM // 2
    scaled = scaled.reshape(row_count, HEADS, HEAD_DIM)
    frequency = jnp.power(10000.0, -jnp.arange(halves).astype(jnp.float32) / halves)
    angles = position[:, None, None] * frequency[None, None, :]
    cosines = jnp.cos(angles)
    sines = jnp.sin(angles)
    front_half = scaled[..., :halves]
    back_half = scaled[..., halves:]
    turned = jnp.concatenate(
        [front_half * cosines - back_half * sines, front_half * sines + back_half * cosines],
        axis=-1,
    )
    return turned.reshape(row_count, ATT).astype(jnp.bfloat16)


def group_parts(queries, key_rows, value_rows):
    row_count = queries.shape[0]
    key_count = key_rows.shape[0]
    query_heads = queries.reshape(row_count, HEADS, HEAD_DIM).transpose(1, 0, 2)
    key_heads = key_rows.reshape(key_count, HEADS, HEAD_DIM).transpose(1, 0, 2)
    value_heads = value_rows.reshape(key_count, HEADS, HEAD_DIM).transpose(1, 0, 2)

    def one_head(operands):
        query_part, key_part, value_part = operands
        scores = jnp.einsum(
            "rd,kd->rk", query_part, key_part, preferred_element_type=jnp.float32
        ) * HEAD_DIM ** (-0.5)
        maxima = jnp.max(scores, axis=-1)
        weights = jnp.exp(scores - maxima[:, None]).astype(jnp.bfloat16)
        totals = jnp.sum(weights.astype(jnp.float32), axis=-1)
        output = jnp.dot(weights, value_part, preferred_element_type=jnp.float32)
        return (output, maxima, totals)

    output, maxima, totals = lax.map(one_head, (query_heads, key_heads, value_heads))
    return (output.transpose(1, 0, 2).reshape(row_count, ATT), maxima.T, totals.T)


def general(
    stream, latents, time_mod, block_mod, w_qkv, qk_gain, w_out, head_mod, w_head, noise_level
):
    slab_count = lax.axis_size("slab")
    seq_count = lax.axis_size("seq")
    slab_index = lax.axis_index("slab")
    seq_index = lax.axis_index("seq")
    group_rows = TOK_DEV * seq_count
    hidden = stream[0].astype(jnp.float32)
    modulation = block_mod + time_mod[0]
    modded = (layer_norm(hidden) * (1.0 + modulation[1]) + modulation[0]).astype(jnp.bfloat16)
    columns = jnp.dot(
        lax.all_gather(modded, "seq", axis=0, tiled=True), w_qkv, preferred_element_type=jnp.float32
    ).astype(jnp.bfloat16)
    own_position = (slab_index * group_rows + seq_index * TOK_DEV + jnp.arange(TOK_DEV)).astype(
        jnp.float32
    )
    full_mixed = lax.all_gather(columns, "seq", axis=1, tiled=True)
    own_mixed = lax.dynamic_slice_in_dim(full_mixed, seq_index * TOK_DEV, TOK_DEV, 0)
    own_queries = norm_rope(own_mixed[:, :ATT], qk_gain[0], own_position)
    group_position = (slab_index * group_rows + jnp.arange(group_rows)).astype(jnp.float32)
    group_keys = norm_rope(full_mixed[:, ATT : 2 * ATT], qk_gain[1], group_position)
    group_values = full_mixed[:, 2 * ATT :]
    all_queries = lax.all_gather(own_queries[None], "slab", axis=0, tiled=True)
    slab_ids = jnp.arange(slab_count)
    output, maxima, totals = group_parts(
        all_queries.reshape(slab_count * TOK_DEV, ATT), group_keys, group_values
    )
    usable = (slab_ids >= slab_index)[:, None, None]
    output = jnp.where(usable, output.reshape(slab_count, TOK_DEV, ATT), 0.0)
    maxima = jnp.where(usable, maxima.reshape(slab_count, TOK_DEV, HEADS), -1e30)
    totals = jnp.where(usable, totals.reshape(slab_count, TOK_DEV, HEADS), 0.0)
    recv_out, recv_max, recv_sum = (
        lax.all_to_all(output, "slab", split_axis=0, concat_axis=0, tiled=True),
        lax.all_to_all(maxima, "slab", split_axis=0, concat_axis=0, tiled=True),
        lax.all_to_all(totals, "slab", split_axis=0, concat_axis=0, tiled=True),
    )
    highest = jnp.max(recv_max, axis=0)
    weights = jnp.exp(recv_max - highest)
    total_sum = jnp.sum(recv_sum * weights, axis=0)
    accum = jnp.sum(
        recv_out.reshape(slab_count, TOK_DEV, HEADS, HEAD_DIM) * weights[..., None], axis=0
    )
    attended = (accum / total_sum[..., None]).reshape(TOK_DEV, ATT).astype(jnp.bfloat16)
    projected = jnp.dot(attended, w_out, preferred_element_type=jnp.float32)
    updated = hidden + modulation[2] * projected
    head_in = (layer_norm(updated) * (1.0 + head_mod[0, 1]) + head_mod[0, 0]).astype(jnp.bfloat16)
    velocity = jnp.dot(head_in, w_head, preferred_element_type=jnp.float32)
    table = sigma_table()
    level_ids = jnp.arange(LEVELS + 1)
    current_level = noise_level[0]
    sigma_now = jnp.sum(jnp.where(level_ids == current_level, table, 0.0))
    sigma_next = jnp.sum(jnp.where(level_ids == current_level - 1, table, 0.0))
    stepped = latents[0] + (sigma_next - sigma_now) * velocity
    moved = from_behind(stepped[None], "slab", -1)
    return (updated.astype(jnp.bfloat16)[None], moved)


def vmem_call(kernel, outs, name, flops, scratch=(), placed=0):
    whole = pl.BlockSpec(memory_space=pltpu.VMEM)
    stay = pl.BlockSpec(memory_space=pltpu.HBM)

    def call(*operands):
        return pl.pallas_call(
            kernel,
            out_shape=[jax.ShapeDtypeStruct(shape, dtype) for shape, dtype in outs],
            in_specs=[whole] * (len(operands) - placed) + [stay] * placed,
            out_specs=[whole] * len(outs),
            scratch_shapes=list(scratch),
            compiler_params=pltpu.CompilerParams(vmem_limit_bytes=VMEM_LIMIT),
            cost_estimate=pl.CostEstimate(flops=flops, bytes_accessed=1 << 20, transcendentals=0),
            name=name,
        )(*operands)

    return call


def here():
    slab, seq = lax.axis_index("slab"), lax.axis_index("seq")
    return seq // 2, seq % 2, slab % 2, slab // 2


def dot_rows(left, right):
    return lax.dot_general(left, right, (((1,), (1,)), ((), ())), preferred_element_type=F32)


def modulated(rows, shift_scale):
    return (layer_norm(rows[...].astype(F32)) * shift_scale[1:2] + shift_scale[0:1]).astype(BF16)


def prepare_kernel(x0, time_mod, block_mod, modded, shift_scale):
    shift_scale[0:1] = block_mod[0:1] + time_mod[0]
    shift_scale[1:2] = 1.0 + (block_mod[1:2] + time_mod[1])
    modded[...] = modulated(x0, shift_scale)


def part_product(modded, weights, part):
    depth = weights.shape[0]
    at = pl.multiple_of(part * depth, depth)
    return jnp.dot(modded[:, pl.ds(at, depth)], weights[...], preferred_element_type=F32)


def project_kernel(
    x1, x2, x3, modded_own, shift_scale, w_own, w_mine, w_last, w_chip,
    w_core, w_core_last, w_core_chip, far_out, near_out, keep_out, sums_out, modded, mixed,
):
    for place, rows in enumerate((x2, x1, x3)):
        modded[place * TOK_DEV : (place + 1) * TOK_DEV, :] = modulated(rows, shift_scale)
    modded[3 * TOK_DEV :, :] = modded_own[...]
    line, side, core, chip = here()
    width = w_own.shape[1]
    own = jnp.dot(modded[...], w_own[...], preferred_element_type=F32).astype(BF16)
    total = part_product(modded, w_mine, 2 * chip + core)
    total += part_product(modded, w_core, 2 * chip + 1 - core)
    total += part_product(modded, w_chip, 2 * (1 - chip) + core)
    total += part_product(modded, w_core_chip, 2 * (1 - chip) + 1 - core)
    total += part_product(modded, w_last, 4 + core)
    other = (total + part_product(modded, w_core_last, 5 - core)).astype(BF16)
    mine = pl.multiple_of(side * width, width)
    there = pl.multiple_of((1 - side) * width, width)
    for place, step in enumerate((2, 1, 3, 0)):
        at = pl.multiple_of(jnp.bitwise_xor(line, step) * TOK_DEV, 16)
        rows = slice(place * TOK_DEV, (place + 1) * TOK_DEV)
        mixed[pl.ds(at, TOK_DEV), pl.ds(mine, width)] = own[rows]
        mixed[pl.ds(at, TOK_DEV), pl.ds(there, width)] = other[rows]
    ones = jnp.ones((16, PAIR), BF16)
    row_id = lax.broadcasted_iota(jnp.int32, (16, ROWS), 0)
    picked = jnp.zeros((16, ROWS), F32)
    for unit in range(3):
        values = mixed[:, unit * PAIR : (unit + 1) * PAIR].astype(F32)
        squares = values * values
        high = squares.astype(BF16)
        low = (squares - high.astype(F32)).astype(BF16)
        total = dot_rows(ones, high) + dot_rows(ones, low)
        kind = (line * 3 + unit) // LINE
        picked += jnp.where(row_id // 3 == kind, total, 0.0)
    picked = jnp.where(row_id < 6, picked, 0.0)
    first = picked.astype(BF16).astype(F32)
    second = (picked - first).astype(BF16).astype(F32)
    third = picked - first - second
    part = row_id % 3
    packed = jnp.where(part == 0, first, jnp.where(part == 1, second, third)).astype(BF16)
    padded = jnp.concatenate([packed, jnp.zeros((16, PAIR - ROWS), BF16)], axis=1)
    sums_out[...] = padded
    near_out[:ROWS, :] = mixed[:, PAIR : 2 * PAIR]
    near_out[ROWS:, :] = padded
    odd = line % 2
    at = pl.multiple_of((1 - odd) * 2 * PAIR, PAIR)
    far_out[:ROWS, :] = mixed[:, pl.ds(at, PAIR)]
    far_out[ROWS:, :] = padded
    at = pl.multiple_of(odd * 2 * PAIR, PAIR)
    keep_out[...] = mixed[:, pl.ds(at, PAIR)]


def step_size(levels):
    level = jnp.broadcast_to(levels[...], (1, HEAD_DIM))

    def sigma(level):
        fraction = level.astype(F32) / LEVELS
        return 5.0 * fraction / (1.0 + 4.0 * fraction)

    return sigma(level - 1) - sigma(level)


def rope_kernel(
    near, far, last_sums, keep, own_sums, gains, cosines, sines, levels, q_out, kv_out, size, units
):
    line, _, _, _ = here()
    upper, odd = line // 2, line % 2
    slots = (
        jnp.where(upper == 1, 2, odd),
        jnp.where((line == 0) | (line == 3), 1, 0),
        jnp.where(upper == 0, 2, 1 - odd),
    )
    units[0] = keep[...]
    units[1] = near[:ROWS, :]
    units[2] = far[:ROWS, :]
    pieces = [
        own_sums[...].astype(F32), near[ROWS:, :].astype(F32),
        far[ROWS:, :].astype(F32), last_sums[...].astype(F32),
    ]
    row_id = lax.broadcasted_iota(jnp.int32, (16, 1), 0)
    cos, sin = cosines[...], sines[...]
    for kind in range(2):
        wanted = row_id // 3 == kind
        total = jnp.zeros((1, PAIR), F32)
        for piece in pieces:
            total += jnp.sum(jnp.where(wanted, piece, 0.0), axis=0, keepdims=True)
        scale = lax.rsqrt(total * (1.0 / ATT) + 1e-06)
        scale = jnp.transpose(jnp.broadcast_to(scale, (HEAD_DIM, PAIR)))[:ROWS]
        values = units[slots[kind]].astype(F32)
        for head in range(2):
            columns = slice(head * HEAD_DIM, (head + 1) * HEAD_DIM)
            at = pl.multiple_of(line * PAIR + head * HEAD_DIM, HEAD_DIM)
            scaled = values[:, columns] * scale * gains[kind : kind + 1, pl.ds(at, HEAD_DIM)]
            turned = scaled * cos + pltpu.roll(scaled, HEAD_DIM // 2, axis=1) * sin
            (kv_out if kind else q_out)[:, columns] = turned.astype(BF16)
    kv_out[:, PAIR:] = units[slots[2]]
    size[...] = step_size(levels)


def attend_group(queries, one, two, head, counts=None):
    columns = slice(head * HEAD_DIM, (head + 1) * HEAD_DIM)
    value_columns = slice(PAIR + head * HEAD_DIM, PAIR + (head + 1) * HEAD_DIM)
    keys = jnp.concatenate([one[:, columns], two[:, columns]], axis=0)
    values = jnp.concatenate([one[:, value_columns], two[:, value_columns]], axis=0)
    ones = jnp.ones((2 * ROWS, HEAD_DIM), BF16)
    scores = dot_rows(queries[:, columns], keys) * HEAD_DIM ** (-0.5)
    maxima = jnp.max(scores, axis=-1, keepdims=True)
    weights = jnp.exp(scores - maxima).astype(BF16)
    output = jnp.dot(weights, jnp.concatenate([values, ones], axis=1), preferred_element_type=F32)
    if counts is not None:
        maxima = jnp.where(counts, maxima, -1e30)
    return output, maxima


def merged(parts):
    highest = functools.reduce(jnp.maximum, [maxima for _, maxima in parts])
    total = sum(output * jnp.exp(maxima - highest) for output, maxima in parts)
    return total, highest


def first_attend_kernel(queries, c0, c1, a0, a1, total_out, highest_out):
    chip = here()[3]
    for head in range(2):
        own = attend_group(queries, a0, a1, head)
        far = attend_group(queries, c0, c1, head, chip == 1)
        total, highest = merged([own, far])
        total_out[head] = total
        highest_out[head] = jnp.broadcast_to(highest, (ROWS, HEAD_DIM))


def last_attend_kernel(
    queries, b0, b1, d0, d1, total_in, highest_in, o3, o2, o1, o0, result
):
    line, _, core, chip = here()
    for head in range(2):
        near = attend_group(queries, b0, b1, head, core == 1)
        far = attend_group(queries, d0, d1, head, chip == 1)
        total, _ = merged([(total_in[head], highest_in[head, :, :1]), near, far])
        columns = slice(head * HEAD_DIM, (head + 1) * HEAD_DIM)
        result[:, columns] = (total[:, :HEAD_DIM] / total[:, HEAD_DIM:]).astype(BF16)
    for step, out in enumerate((o0, o1, o2, o3)):
        at = pl.multiple_of(jnp.bitwise_xor(line, step) * TOK_DEV, 16)
        out[...] = result[pl.ds(at, TOK_DEV), :]


def load(sources, held, arrived):
    copies = [
        pltpu.make_async_copy(source, target, arrived.at[i])
        for i, (source, target) in enumerate(zip(sources, held))
    ]
    for copy in copies:
        copy.start()
    return copies


def times_w_out(rows, w_out, step):
    at = pl.multiple_of(jnp.bitwise_xor(here()[0], step) * PAIR, PAIR)
    return jnp.dot(rows[...], w_out[pl.ds(at, PAIR), :], preferred_element_type=F32)


def begin_kernel(
    r0, w_out, stream_in, time_in, block_in, head_in, base, vectors,
    stream, time_mod, block_mod, head_mod, arrived,
):
    copies = load(
        (stream_in, time_in, block_in, head_in), (stream, time_mod, block_mod, head_mod), arrived
    )
    projected = times_w_out(r0, w_out, 0)
    for copy in copies:
        copy.wait()
    gate = block_mod[2:3] + time_mod[2]
    base[...] = stream[...].astype(F32) + gate * projected
    vectors[0:1] = gate
    vectors[1:2] = 1.0 + head_mod[1:2]
    vectors[2:3] = head_mod[0:1]


def finish_kernel(
    r2, r3, r1, w_out, base, vectors, w_head, size, latents_in, stream_out, latents_out,
    latents, arrived,
):
    copies = load((latents_in,), (latents,), arrived)
    projected = times_w_out(r3, w_out, 3) + times_w_out(r2, w_out, 2) + times_w_out(r1, w_out, 1)
    updated = base[...] + vectors[0:1] * projected
    stream_out[...] = updated
    head_in = (layer_norm(updated) * vectors[1:2] + vectors[2:3]).astype(BF16)
    velocity = dot_rows(head_in, w_head[...])

    copies[0].wait()
    latents_out[...] = latents[...] + size[0:1, :CHAN] * velocity


def lines(
    stream, latents, time_mod, block_mod, w_qkv, qk_gain, w_out, head_mod, w_head, noise_level
):
    slab, seq = lax.axis_index("slab"), lax.axis_index("seq")
    side, core = seq % 2, slab % 2

    def along(step, value):
        return lax.ppermute(value, "seq", [(i, i ^ (2 * step)) for i in range(2 * LINE)])

    def across(value):
        return lax.ppermute(value, "seq", [(i, i ^ 1) for i in range(2 * LINE)])

    def cores(value):
        return lax.ppermute(value, "slab", [(i, i ^ 1) for i in range(4)])

    def chips(value):
        return lax.ppermute(value, "slab", [(i, i ^ 2) for i in range(4)])

    def chips_and_sides(value):
        count = 2 * LINE
        pairs = [
            (s * count + i, (s ^ 2) * count + (i ^ 1 if s < 2 else i))
            for s in range(4)
            for i in range(count)
        ]
        return lax.ppermute(value, ("slab", "seq"), pairs)

    rows = stream[0]
    time_rows = time_mod.transpose(1, 0, 2)
    depth = D // 6
    half_mine = lax.dynamic_slice_in_dim(w_qkv, slab * depth, depth, 0)
    half_last = lax.dynamic_slice_in_dim(w_qkv, (4 + core) * depth, depth, 0)
    w_mine, w_last = across(half_mine), across(half_last)
    late_rows, _ = lax.optimization_barrier((rows, half_mine))
    x1, x2, x3 = along(1, rows), along(2, rows), along(3, rows)

    at = (jnp.arange(LINE)[:, None] * 2 + side) * TOK_DEV + jnp.arange(TOK_DEV)[None]
    position = (slab * (2 * LINE * TOK_DEV) + at.reshape(ROWS)).astype(F32)
    halves = HEAD_DIM // 2
    frequency = jnp.power(10000.0, -jnp.arange(halves).astype(F32) / halves)
    angles = position[:, None] * frequency[None]
    cosines, sines = jnp.cos(angles), jnp.sin(angles)
    cosines = jnp.concatenate([cosines, cosines], axis=1)
    sines = jnp.concatenate([-sines, sines], axis=1)
    modded_own, shift_scale = vmem_call(
        prepare_kernel, [((TOK_DEV, D), BF16), ((2, D), F32)], "prepare", 1 << 20
    )(rows, time_rows, block_mod)
    w_chip = chips(w_mine)
    w_last, modded_own, shift_scale = lax.optimization_barrier((w_last, modded_own, shift_scale))
    w_core_last = cores(w_last)
    w_mine, w_chip = lax.optimization_barrier((w_mine, w_chip))
    w_core, w_core_chip = cores(w_mine), cores(w_chip)
    message = (ROWS + 16, PAIR)
    far, near, keep, sums = vmem_call(
        project_kernel,
        [(message, BF16), (message, BF16), ((ROWS, PAIR), BF16), ((16, PAIR), BF16)],
        "project", 1 << 28, [pltpu.VMEM((ROWS, D), BF16), pltpu.VMEM((ROWS, 3 * PAIR), BF16)],
    )(
        x1, x2, x3, modded_own, shift_scale, w_qkv,
        w_mine, w_last, w_chip, w_core, w_core_last, w_core_chip,
    )
    far, last_sums, near = along(2, far), along(3, sums), along(1, near)
    queries, pairs, size = vmem_call(
        rope_kernel,
        [((ROWS, PAIR), BF16), ((ROWS, 2 * PAIR), BF16), ((1, HEAD_DIM), F32)],
        "rope", 1 << 22, [pltpu.VMEM((3, ROWS, PAIR), BF16)],
    )(near, far, last_sums, keep, sums, qk_gain, cosines, sines, noise_level[None])
    chip_pairs, side_pairs = chips(pairs), across(pairs)
    both_pairs = chips_and_sides(pairs)
    chip_pairs, side_pairs = lax.optimization_barrier((chip_pairs, side_pairs))
    state = [((2, ROWS, PAIR), F32), ((2, ROWS, HEAD_DIM), F32)]
    now = vmem_call(first_attend_kernel, state, "attend_first", 1 << 27)(
        queries, chip_pairs, both_pairs, pairs, side_pairs
    )
    _, late_pairs = lax.optimization_barrier((side_pairs, pairs))
    core_pairs = cores(late_pairs)
    core_side, core_chip, core_both = cores(side_pairs), cores(chip_pairs), cores(both_pairs)
    part3, part2, part1, part0 = vmem_call(
        last_attend_kernel, [((TOK_DEV, PAIR), BF16)] * 4, "attend_last", 1 << 27,
        [pltpu.VMEM((ROWS, PAIR), BF16)],
    )(queries, core_pairs, core_side, core_chip, core_both, *now)
    late = [along(2, part2), along(3, part3), along(1, part1)]
    loaded = (rows, time_rows, block_mod, head_mod[0])
    base, vectors = vmem_call(
        begin_kernel, [((TOK_DEV, D), F32), ((8, D), F32)], "begin", 1 << 28,
        [pltpu.VMEM(v.shape, v.dtype) for v in loaded] + [pltpu.SemaphoreType.DMA((len(loaded),))],
        placed=len(loaded),
    )(part0, w_out, *loaded)
    updated, stepped = vmem_call(
        finish_kernel, [((TOK_DEV, D), F32), ((TOK_DEV, CHAN), F32)], "finish", 1 << 28,
        [pltpu.VMEM((TOK_DEV, CHAN), F32), pltpu.SemaphoreType.DMA((1,))], placed=1,
    )(*late, w_out, base, vectors, w_head.T, size, latents[0])
    return (updated.astype(BF16)[None], from_behind(stepped[None], "slab", -1))


def solution(mesh):
    in_specs = (
        P("slab", "seq", None),
        P("slab", "seq", None),
        P("slab", None, None),
        P(),
        P(None, "seq"),
        P(),
        P(),
        P("slab", None, None),
        P(),
        P("slab"),
    )
    out_specs = (P("slab", "seq", None), P("slab", "seq", None))
    local = lines if tuple(mesh.shape.values()) == (4, 2 * LINE) else general
    return jax.shard_map(local, mesh=mesh, in_specs=in_specs, out_specs=out_specs, check_vma=False)
```

```python
import functools

import jax
import jax.numpy as jnp
from jax import lax
from jax.experimental import pallas as pl
from jax.experimental.pallas import tpu as pltpu
from jax.sharding import PartitionSpec as P

HEADS = 8
HEAD_DIM = 128
LEVELS = 32
TOK_DEV = 48
ATT = 1024
D = 1536
CHAN = 64
PAIR = 2 * HEAD_DIM
LINE = 4
ROWS = LINE * TOK_DEV
BF16 = jnp.bfloat16
F32 = jnp.float32
VMEM_LIMIT = 40 * 1024 * 1024
EXPONENT = HEAD_DIM ** (-0.5) * 1.4426950408889634


def from_behind(value, axis, steps):
    count = lax.axis_size(axis)
    pairs = [(source, (source + steps) % count) for source in range(count)]
    return lax.ppermute(value, axis, pairs)


def layer_norm(values):
    center = values - jnp.mean(values, axis=-1, keepdims=True)
    spread = jnp.mean(center * center, axis=-1, keepdims=True)
    return center * lax.rsqrt(spread + 1e-06)


def sigma_table():
    fraction = jnp.arange(LEVELS + 1).astype(jnp.float32) / LEVELS
    return 5.0 * fraction / (1.0 + 4.0 * fraction)


def norm_rope(values, gain_row, position):
    row_count = values.shape[0]
    floats = values.astype(jnp.float32)
    scaled = (
        floats * lax.rsqrt(jnp.mean(floats * floats, axis=-1, keepdims=True) + 1e-06) * gain_row
    )
    halves = HEAD_DIM // 2
    scaled = scaled.reshape(row_count, HEADS, HEAD_DIM)
    frequency = jnp.power(10000.0, -jnp.arange(halves).astype(jnp.float32) / halves)
    angles = position[:, None, None] * frequency[None, None, :]
    cosines = jnp.cos(angles)
    sines = jnp.sin(angles)
    front_half = scaled[..., :halves]
    back_half = scaled[..., halves:]
    turned = jnp.concatenate(
        [front_half * cosines - back_half * sines, front_half * sines + back_half * cosines],
        axis=-1,
    )
    return turned.reshape(row_count, ATT).astype(jnp.bfloat16)


def group_parts(queries, key_rows, value_rows):
    row_count = queries.shape[0]
    key_count = key_rows.shape[0]
    query_heads = queries.reshape(row_count, HEADS, HEAD_DIM).transpose(1, 0, 2)
    key_heads = key_rows.reshape(key_count, HEADS, HEAD_DIM).transpose(1, 0, 2)
    value_heads = value_rows.reshape(key_count, HEADS, HEAD_DIM).transpose(1, 0, 2)

    def one_head(operands):
        query_part, key_part, value_part = operands
        scores = jnp.einsum(
            "rd,kd->rk", query_part, key_part, preferred_element_type=jnp.float32
        ) * HEAD_DIM ** (-0.5)
        maxima = jnp.max(scores, axis=-1)
        weights = jnp.exp(scores - maxima[:, None]).astype(jnp.bfloat16)
        totals = jnp.sum(weights.astype(jnp.float32), axis=-1)
        output = jnp.dot(weights, value_part, preferred_element_type=jnp.float32)
        return (output, maxima, totals)

    output, maxima, totals = lax.map(one_head, (query_heads, key_heads, value_heads))
    return (output.transpose(1, 0, 2).reshape(row_count, ATT), maxima.T, totals.T)


def general(
    stream, latents, time_mod, block_mod, w_qkv, qk_gain, w_out, head_mod, w_head, noise_level
):
    slab_count = lax.axis_size("slab")
    seq_count = lax.axis_size("seq")
    slab_index = lax.axis_index("slab")
    seq_index = lax.axis_index("seq")
    group_rows = TOK_DEV * seq_count
    hidden = stream[0].astype(jnp.float32)
    modulation = block_mod + time_mod[0]
    modded = (layer_norm(hidden) * (1.0 + modulation[1]) + modulation[0]).astype(jnp.bfloat16)
    columns = jnp.dot(
        lax.all_gather(modded, "seq", axis=0, tiled=True), w_qkv, preferred_element_type=jnp.float32
    ).astype(jnp.bfloat16)
    own_position = (slab_index * group_rows + seq_index * TOK_DEV + jnp.arange(TOK_DEV)).astype(
        jnp.float32
    )
    full_mixed = lax.all_gather(columns, "seq", axis=1, tiled=True)
    own_mixed = lax.dynamic_slice_in_dim(full_mixed, seq_index * TOK_DEV, TOK_DEV, 0)
    own_queries = norm_rope(own_mixed[:, :ATT], qk_gain[0], own_position)
    group_position = (slab_index * group_rows + jnp.arange(group_rows)).astype(jnp.float32)
    group_keys = norm_rope(full_mixed[:, ATT : 2 * ATT], qk_gain[1], group_position)
    group_values = full_mixed[:, 2 * ATT :]
    all_queries = lax.all_gather(own_queries[None], "slab", axis=0, tiled=True)
    slab_ids = jnp.arange(slab_count)
    output, maxima, totals = group_parts(
        all_queries.reshape(slab_count * TOK_DEV, ATT), group_keys, group_values
    )
    usable = (slab_ids >= slab_index)[:, None, None]
    output = jnp.where(usable, output.reshape(slab_count, TOK_DEV, ATT), 0.0)
    maxima = jnp.where(usable, maxima.reshape(slab_count, TOK_DEV, HEADS), -1e30)
    totals = jnp.where(usable, totals.reshape(slab_count, TOK_DEV, HEADS), 0.0)
    recv_out, recv_max, recv_sum = (
        lax.all_to_all(output, "slab", split_axis=0, concat_axis=0, tiled=True),
        lax.all_to_all(maxima, "slab", split_axis=0, concat_axis=0, tiled=True),
        lax.all_to_all(totals, "slab", split_axis=0, concat_axis=0, tiled=True),
    )
    highest = jnp.max(recv_max, axis=0)
    weights = jnp.exp(recv_max - highest)
    total_sum = jnp.sum(recv_sum * weights, axis=0)
    accum = jnp.sum(
        recv_out.reshape(slab_count, TOK_DEV, HEADS, HEAD_DIM) * weights[..., None], axis=0
    )
    attended = (accum / total_sum[..., None]).reshape(TOK_DEV, ATT).astype(jnp.bfloat16)
    projected = jnp.dot(attended, w_out, preferred_element_type=jnp.float32)
    updated = hidden + modulation[2] * projected
    head_in = (layer_norm(updated) * (1.0 + head_mod[0, 1]) + head_mod[0, 0]).astype(jnp.bfloat16)
    velocity = jnp.dot(head_in, w_head, preferred_element_type=jnp.float32)
    table = sigma_table()
    level_ids = jnp.arange(LEVELS + 1)
    current_level = noise_level[0]
    sigma_now = jnp.sum(jnp.where(level_ids == current_level, table, 0.0))
    sigma_next = jnp.sum(jnp.where(level_ids == current_level - 1, table, 0.0))
    stepped = latents[0] + (sigma_next - sigma_now) * velocity
    moved = from_behind(stepped[None], "slab", -1)
    return (updated.astype(jnp.bfloat16)[None], moved)


def vmem_call(kernel, outs, name, flops, scratch=(), placed=0):
    whole = pl.BlockSpec(memory_space=pltpu.VMEM)
    stay = pl.BlockSpec(memory_space=pltpu.HBM)

    def call(*operands):
        return pl.pallas_call(
            kernel,
            out_shape=[jax.ShapeDtypeStruct(shape, dtype) for shape, dtype in outs],
            in_specs=[whole] * (len(operands) - placed) + [stay] * placed,
            out_specs=[whole] * len(outs),
            scratch_shapes=list(scratch),
            compiler_params=pltpu.CompilerParams(vmem_limit_bytes=VMEM_LIMIT),
            cost_estimate=pl.CostEstimate(flops=flops, bytes_accessed=1 << 20, transcendentals=0),
            name=name,
        )(*operands)

    return call


def here():
    slab, seq = lax.axis_index("slab"), lax.axis_index("seq")
    return seq // 2, seq % 2, slab % 2, slab // 2


def dot_rows(left, right):
    return lax.dot_general(left, right, (((1,), (1,)), ((), ())), preferred_element_type=F32)


def modulated(rows, shift_scale):
    return (layer_norm(rows[...].astype(F32)) * shift_scale[1:2] + shift_scale[0:1]).astype(BF16)


def prepare_kernel(x0, time_mod, block_mod, modded, shift_scale):
    shift_scale[0:1] = block_mod[0:1] + time_mod[0]
    shift_scale[1:2] = 1.0 + (block_mod[1:2] + time_mod[1])
    modded[...] = modulated(x0, shift_scale)


def part_product(modded, weights, part):
    depth = weights.shape[0]
    at = pl.multiple_of(part * depth, depth)
    return jnp.dot(modded[:, pl.ds(at, depth)], weights[...], preferred_element_type=F32)


def project_kernel(
    x1, x2, x3, modded_own, shift_scale, w_own, w_mine, w_last, w_chip,
    w_core, w_core_last, w_core_chip, far_out, near_out, keep_out, sums_out, modded, mixed,
):
    for place, rows in enumerate((x2, x1, x3)):
        modded[place * TOK_DEV : (place + 1) * TOK_DEV, :] = modulated(rows, shift_scale)
    modded[3 * TOK_DEV :, :] = modded_own[...]
    line, side, core, chip = here()
    width = w_own.shape[1]
    own = jnp.dot(modded[...], w_own[...], preferred_element_type=F32).astype(BF16)
    total = part_product(modded, w_mine, 2 * chip + core)
    total += part_product(modded, w_core, 2 * chip + 1 - core)
    total += part_product(modded, w_chip, 2 * (1 - chip) + core)
    total += part_product(modded, w_core_chip, 2 * (1 - chip) + 1 - core)
    total += part_product(modded, w_last, 4 + core)
    other = (total + part_product(modded, w_core_last, 5 - core)).astype(BF16)
    mine = pl.multiple_of(side * width, width)
    there = pl.multiple_of((1 - side) * width, width)
    for place, step in enumerate((2, 1, 3, 0)):
        at = pl.multiple_of(jnp.bitwise_xor(line, step) * TOK_DEV, 16)
        rows = slice(place * TOK_DEV, (place + 1) * TOK_DEV)
        mixed[pl.ds(at, TOK_DEV), pl.ds(mine, width)] = own[rows]
        mixed[pl.ds(at, TOK_DEV), pl.ds(there, width)] = other[rows]
    ones = jnp.ones((16, PAIR), BF16)
    row_id = lax.broadcasted_iota(jnp.int32, (16, ROWS), 0)
    picked = jnp.zeros((16, ROWS), F32)
    for unit in range(3):
        values = mixed[:, unit * PAIR : (unit + 1) * PAIR].astype(F32)
        squares = values * values
        high = squares.astype(BF16)
        low = (squares - high.astype(F32)).astype(BF16)
        total = dot_rows(ones, high) + dot_rows(ones, low)
        kind = (line * 3 + unit) // LINE
        picked += jnp.where(row_id // 3 == kind, total, 0.0)
    picked = jnp.where(row_id < 6, picked, 0.0)
    first = picked.astype(BF16).astype(F32)
    second = (picked - first).astype(BF16).astype(F32)
    third = picked - first - second
    part = row_id % 3
    packed = jnp.where(part == 0, first, jnp.where(part == 1, second, third)).astype(BF16)
    padded = jnp.concatenate([packed, jnp.zeros((16, PAIR - ROWS), BF16)], axis=1)
    sums_out[...] = padded
    near_out[:ROWS, :] = mixed[:, PAIR : 2 * PAIR]
    near_out[ROWS:, :] = padded
    odd = line % 2
    at = pl.multiple_of((1 - odd) * 2 * PAIR, PAIR)
    far_out[:ROWS, :] = mixed[:, pl.ds(at, PAIR)]
    far_out[ROWS:, :] = padded
    at = pl.multiple_of(odd * 2 * PAIR, PAIR)
    keep_out[...] = mixed[:, pl.ds(at, PAIR)]


def step_size(levels):
    level = jnp.broadcast_to(levels[...], (1, HEAD_DIM))

    def sigma(level):
        fraction = level.astype(F32) / LEVELS
        return 5.0 * fraction / (1.0 + 4.0 * fraction)

    return sigma(level - 1) - sigma(level)


def row_scale(pieces, kind):
    wanted = lax.broadcasted_iota(jnp.int32, (16, 1), 0) // 3 == kind
    total = jnp.zeros((1, PAIR), F32)
    for piece in pieces:
        total += jnp.sum(jnp.where(wanted, piece, 0.0), axis=0, keepdims=True)
    scale = lax.rsqrt(total * (1.0 / ATT) + 1e-06)
    return jnp.transpose(jnp.broadcast_to(scale, (HEAD_DIM, PAIR)))[:ROWS]


def turn(values, scale, gains, kind, head, cos, sin):
    columns = slice(head * HEAD_DIM, (head + 1) * HEAD_DIM)
    at = pl.multiple_of(here()[0] * PAIR + head * HEAD_DIM, HEAD_DIM)
    scaled = values[:, columns] * scale * gains[kind : kind + 1, pl.ds(at, HEAD_DIM)]
    return (scaled * cos + pltpu.roll(scaled, HEAD_DIM // 2, axis=1) * sin).astype(BF16)


def keys_kernel(
    near, far, middle_sums, keep, own_sums, gains, cosines, sines, levels,
    kv_out, q_out, sums_out, size, units,
):
    line, _, _, _ = here()
    upper, odd = line // 2, line % 2
    slots = (
        jnp.where(upper == 1, 2, odd),
        jnp.where((line == 0) | (line == 3), 1, 0),
        jnp.where(upper == 0, 2, 1 - odd),
    )
    units[0] = keep[...]
    units[1] = near[:ROWS, :]
    units[2] = far[:ROWS, :]
    inner = (line == 1) | (line == 2)
    pieces = [
        own_sums[...].astype(F32), near[ROWS:, :].astype(F32), far[ROWS:, :].astype(F32),
        jnp.where(inner, middle_sums[...].astype(F32), 0.0),
    ]
    scale = row_scale(pieces, 1)
    values = units[slots[1]].astype(F32)
    for head in range(2):
        columns = slice(head * HEAD_DIM, (head + 1) * HEAD_DIM)
        kv_out[:, columns] = turn(values, scale, gains, 1, head, cosines[...], sines[...])
    kv_out[:, PAIR:] = units[slots[2]]
    size[...] = step_size(levels)
    q_out[...] = units[slots[0]]
    sums_out[...] = pieces[0] + pieces[1] + pieces[2] + pieces[3]


def queries_kernel(raw, sums, last_sums, gains, cosines, sines, q_out):
    line = here()[0]
    last = jnp.where(line == 3, last_sums[...].astype(F32), 0.0)
    scale = row_scale([sums[...], last], 0)
    values = raw[...].astype(F32)
    for head in range(2):
        columns = slice(head * HEAD_DIM, (head + 1) * HEAD_DIM)
        q_out[:, columns] = turn(values, scale, gains, 0, head, cosines[...], sines[...])


def attend_group(queries, one, two, head, counts=None):
    columns = slice(head * HEAD_DIM, (head + 1) * HEAD_DIM)
    value_columns = slice(PAIR + head * HEAD_DIM, PAIR + (head + 1) * HEAD_DIM)
    keys = jnp.concatenate([one[:, columns], two[:, columns]], axis=0)
    values = jnp.concatenate([one[:, value_columns], two[:, value_columns]], axis=0)
    ones = jnp.ones((2 * ROWS, HEAD_DIM), BF16)
    scores = dot_rows(queries[:, columns], keys) * HEAD_DIM ** (-0.5)
    maxima = jnp.max(scores, axis=-1, keepdims=True)
    weights = jnp.exp(scores - maxima).astype(BF16)
    output = jnp.dot(weights, jnp.concatenate([values, ones], axis=1), preferred_element_type=F32)
    if counts is not None:
        maxima = jnp.where(counts, maxima, -1e30)
    return output, maxima


def merged(parts):
    highest = functools.reduce(jnp.maximum, [maxima for _, maxima in parts])
    total = sum(output * jnp.exp(maxima - highest) for output, maxima in parts)
    return total, highest


def first_attend_kernel(queries, c0, c1, a0, a1, total_out, highest_out):
    chip = here()[3]
    for head in range(2):
        own = attend_group(queries, a0, a1, head)
        far = attend_group(queries, c0, c1, head, chip == 1)
        total, highest = merged([own, far])
        total_out[head] = total
        highest_out[head] = jnp.broadcast_to(highest, (ROWS, HEAD_DIM))


def last_attend_kernel(
    queries, b0, b1, d0, d1, total_in, highest_in, o3, o2, o1, o0, result
):
    line, _, core, chip = here()
    for head in range(2):
        near = attend_group(queries, b0, b1, head, core == 1)
        far = attend_group(queries, d0, d1, head, chip == 1)
        total, _ = merged([(total_in[head], highest_in[head, :, :1]), near, far])
        columns = slice(head * HEAD_DIM, (head + 1) * HEAD_DIM)
        result[:, columns] = (total[:, :HEAD_DIM] / total[:, HEAD_DIM:]).astype(BF16)
    for step, out in enumerate((o0, o1, o2, o3)):
        at = pl.multiple_of(jnp.bitwise_xor(line, step) * TOK_DEV, 16)
        out[...] = result[pl.ds(at, TOK_DEV), :]


def load(sources, held, arrived):
    copies = [
        pltpu.make_async_copy(source, target, arrived.at[i])
        for i, (source, target) in enumerate(zip(sources, held))
    ]
    for copy in copies:
        copy.start()
    return copies


def times_w_out(rows, w_out, step):
    at = pl.multiple_of(jnp.bitwise_xor(here()[0], step) * PAIR, PAIR)
    return jnp.dot(rows[...], w_out[pl.ds(at, PAIR), :], preferred_element_type=F32)


def begin_kernel(
    r0, w_out, stream_in, time_in, block_in, head_in, base, vectors,
    stream, time_mod, block_mod, head_mod, arrived,
):
    copies = load(
        (stream_in, time_in, block_in, head_in), (stream, time_mod, block_mod, head_mod), arrived
    )
    projected = times_w_out(r0, w_out, 0)
    for copy in copies:
        copy.wait()
    gate = block_mod[2:3] + time_mod[2]
    base[...] = stream[...].astype(F32) + gate * projected
    vectors[0:1] = gate
    vectors[1:2] = 1.0 + head_mod[1:2]
    vectors[2:3] = head_mod[0:1]


def finish_kernel(
    r2, r3, r1, w_out, base, vectors, w_head, size, latents_in, stream_out, latents_out,
    latents, arrived,
):
    copies = load((latents_in,), (latents,), arrived)
    projected = times_w_out(r3, w_out, 3) + times_w_out(r2, w_out, 2) + times_w_out(r1, w_out, 1)
    updated = base[...] + vectors[0:1] * projected
    stream_out[...] = updated
    head_in = (layer_norm(updated) * vectors[1:2] + vectors[2:3]).astype(BF16)
    velocity = dot_rows(head_in, w_head[...])

    copies[0].wait()
    latents_out[...] = latents[...] + size[0:1, :CHAN] * velocity


def lines(
    stream, latents, time_mod, block_mod, w_qkv, qk_gain, w_out, head_mod, w_head, noise_level
):
    slab, seq = lax.axis_index("slab"), lax.axis_index("seq")
    side, core = seq % 2, slab % 2

    def along(step, value):
        return lax.ppermute(value, "seq", [(i, i ^ (2 * step)) for i in range(2 * LINE)])

    def middle(value):
        pairs = [(i, i ^ 6 if i in (2, 3, 4, 5) else i ^ 1) for i in range(2 * LINE)]
        return lax.ppermute(value, "seq", pairs)

    def across(value):
        return lax.ppermute(value, "seq", [(i, i ^ 1) for i in range(2 * LINE)])

    def cores(value):
        return lax.ppermute(value, "slab", [(i, i ^ 1) for i in range(4)])

    def chips(value):
        return lax.ppermute(value, "slab", [(i, i ^ 2) for i in range(4)])

    def chips_and_sides(value):
        count = 2 * LINE
        pairs = [
            (s * count + i, (s ^ 2) * count + (i ^ 1 if s < 2 else i))
            for s in range(4)
            for i in range(count)
        ]
        return lax.ppermute(value, ("slab", "seq"), pairs)

    rows = stream[0]
    time_rows = time_mod.transpose(1, 0, 2)
    depth = D // 6
    half_mine = lax.dynamic_slice_in_dim(w_qkv, slab * depth, depth, 0)
    half_last = lax.dynamic_slice_in_dim(w_qkv, (4 + core) * depth, depth, 0)
    w_mine, w_last = across(half_mine), across(half_last)
    late_rows, _ = lax.optimization_barrier((rows, half_mine))
    x1, x2, x3 = along(1, rows), along(2, rows), along(3, rows)

    at = (jnp.arange(LINE)[:, None] * 2 + side) * TOK_DEV + jnp.arange(TOK_DEV)[None]
    position = (slab * (2 * LINE * TOK_DEV) + at.reshape(ROWS)).astype(F32)
    halves = HEAD_DIM // 2
    frequency = jnp.power(10000.0, -jnp.arange(halves).astype(F32) / halves)
    angles = position[:, None] * frequency[None]
    cosines, sines = jnp.cos(angles), jnp.sin(angles)
    cosines = jnp.concatenate([cosines, cosines], axis=1)
    sines = jnp.concatenate([-sines, sines], axis=1)
    modded_own, shift_scale = vmem_call(
        prepare_kernel, [((TOK_DEV, D), BF16), ((2, D), F32)], "prepare", 1 << 20
    )(rows, time_rows, block_mod)
    w_chip = chips(w_mine)
    w_last, modded_own, shift_scale = lax.optimization_barrier((w_last, modded_own, shift_scale))
    w_core_last = cores(w_last)
    w_mine, w_chip = lax.optimization_barrier((w_mine, w_chip))
    w_core, w_core_chip = cores(w_mine), cores(w_chip)
    message = (ROWS + 16, PAIR)
    far, near, keep, sums = vmem_call(
        project_kernel,
        [(message, BF16), (message, BF16), ((ROWS, PAIR), BF16), ((16, PAIR), BF16)],
        "project", 1 << 28, [pltpu.VMEM((ROWS, D), BF16), pltpu.VMEM((ROWS, 3 * PAIR), BF16)],
    )(
        x1, x2, x3, modded_own, shift_scale, w_qkv,
        w_mine, w_last, w_chip, w_core, w_core_last, w_core_chip,
    )
    near, middle_sums, far = along(1, near), middle(sums), along(2, far)
    pairs, raw_queries, some_sums, size = vmem_call(
        keys_kernel,
        [((ROWS, 2 * PAIR), BF16), ((ROWS, PAIR), BF16), ((16, PAIR), F32), ((1, HEAD_DIM), F32)],
        "rope_keys", 1 << 22, [pltpu.VMEM((3, ROWS, PAIR), BF16)],
    )(near, far, middle_sums, keep, sums, qk_gain, cosines, sines, noise_level[None])
    _, late_sums = lax.optimization_barrier((some_sums, sums))
    chip_pairs, side_pairs, last_sums = chips(pairs), across(pairs), along(3, late_sums)
    both_pairs = chips_and_sides(pairs)
    chip_pairs, side_pairs = lax.optimization_barrier((chip_pairs, side_pairs))
    both_pairs, last_sums = lax.optimization_barrier((both_pairs, last_sums))
    (queries,) = vmem_call(queries_kernel, [((ROWS, PAIR), BF16)], "rope_queries", 1 << 22)(
        raw_queries, some_sums, last_sums, qk_gain, cosines, sines
    )
    state = [((2, ROWS, PAIR), F32), ((2, ROWS, HEAD_DIM), F32)]
    now = vmem_call(first_attend_kernel, state, "attend_first", 1 << 27)(
        queries, chip_pairs, both_pairs, pairs, side_pairs
    )
    core_pairs = cores(pairs)
    core_side, core_chip, core_both = cores(side_pairs), cores(chip_pairs), cores(both_pairs)
    part3, part2, part1, part0 = vmem_call(
        last_attend_kernel, [((TOK_DEV, PAIR), BF16)] * 4, "attend_last", 1 << 27,
        [pltpu.VMEM((ROWS, PAIR), BF16)],
    )(queries, core_pairs, core_side, core_chip, core_both, *now)
    late = [along(2, part2), along(3, part3), along(1, part1)]
    loaded = (rows, time_rows, block_mod, head_mod[0])
    base, vectors = vmem_call(
        begin_kernel, [((TOK_DEV, D), F32), ((8, D), F32)], "begin", 1 << 28,
        [pltpu.VMEM(v.shape, v.dtype) for v in loaded] + [pltpu.SemaphoreType.DMA((len(loaded),))],
        placed=len(loaded),
    )(part0, w_out, *loaded)
    updated, stepped = vmem_call(
        finish_kernel, [((TOK_DEV, D), F32), ((TOK_DEV, CHAN), F32)], "finish", 1 << 28,
        [pltpu.VMEM((TOK_DEV, CHAN), F32), pltpu.SemaphoreType.DMA((1,))], placed=1,
    )(*late, w_out, base, vectors, w_head.T, size, latents[0])
    return (updated.astype(BF16)[None], from_behind(stepped[None], "slab", -1))


def solution(mesh):
    in_specs = (
        P("slab", "seq", None),
        P("slab", "seq", None),
        P("slab", None, None),
        P(),
        P(None, "seq"),
        P(),
        P(),
        P("slab", None, None),
        P(),
        P("slab"),
    )
    out_specs = (P("slab", "seq", None), P("slab", "seq", None))
    local = lines if tuple(mesh.shape.values()) == (4, 2 * LINE) else general
    return jax.shard_map(local, mesh=mesh, in_specs=in_specs, out_specs=out_specs, check_vma=False)
```

```python
import functools

import jax
import jax.numpy as jnp
from jax import lax
from jax.experimental import pallas as pl
from jax.experimental.pallas import tpu as pltpu
from jax.sharding import PartitionSpec as P

HEADS = 8
HEAD_DIM = 128
LEVELS = 32
TOK_DEV = 48
ATT = 1024
D = 1536
CHAN = 64
PAIR = 2 * HEAD_DIM
LINE = 4
ROWS = LINE * TOK_DEV
BF16 = jnp.bfloat16
F32 = jnp.float32
VMEM_LIMIT = 40 * 1024 * 1024
EXPONENT = HEAD_DIM ** (-0.5) * 1.4426950408889634


def from_behind(value, axis, steps):
    count = lax.axis_size(axis)
    pairs = [(source, (source + steps) % count) for source in range(count)]
    return lax.ppermute(value, axis, pairs)


def layer_norm(values):
    center = values - jnp.mean(values, axis=-1, keepdims=True)
    spread = jnp.mean(center * center, axis=-1, keepdims=True)
    return center * lax.rsqrt(spread + 1e-06)


def sigma_table():
    fraction = jnp.arange(LEVELS + 1).astype(jnp.float32) / LEVELS
    return 5.0 * fraction / (1.0 + 4.0 * fraction)


def norm_rope(values, gain_row, position):
    row_count = values.shape[0]
    floats = values.astype(jnp.float32)
    scaled = (
        floats * lax.rsqrt(jnp.mean(floats * floats, axis=-1, keepdims=True) + 1e-06) * gain_row
    )
    halves = HEAD_DIM // 2
    scaled = scaled.reshape(row_count, HEADS, HEAD_DIM)
    frequency = jnp.power(10000.0, -jnp.arange(halves).astype(jnp.float32) / halves)
    angles = position[:, None, None] * frequency[None, None, :]
    cosines = jnp.cos(angles)
    sines = jnp.sin(angles)
    front_half = scaled[..., :halves]
    back_half = scaled[..., halves:]
    turned = jnp.concatenate(
        [front_half * cosines - back_half * sines, front_half * sines + back_half * cosines],
        axis=-1,
    )
    return turned.reshape(row_count, ATT).astype(jnp.bfloat16)


def group_parts(queries, key_rows, value_rows):
    row_count = queries.shape[0]
    key_count = key_rows.shape[0]
    query_heads = queries.reshape(row_count, HEADS, HEAD_DIM).transpose(1, 0, 2)
    key_heads = key_rows.reshape(key_count, HEADS, HEAD_DIM).transpose(1, 0, 2)
    value_heads = value_rows.reshape(key_count, HEADS, HEAD_DIM).transpose(1, 0, 2)

    def one_head(operands):
        query_part, key_part, value_part = operands
        scores = jnp.einsum(
            "rd,kd->rk", query_part, key_part, preferred_element_type=jnp.float32
        ) * HEAD_DIM ** (-0.5)
        maxima = jnp.max(scores, axis=-1)
        weights = jnp.exp(scores - maxima[:, None]).astype(jnp.bfloat16)
        totals = jnp.sum(weights.astype(jnp.float32), axis=-1)
        output = jnp.dot(weights, value_part, preferred_element_type=jnp.float32)
        return (output, maxima, totals)

    output, maxima, totals = lax.map(one_head, (query_heads, key_heads, value_heads))
    return (output.transpose(1, 0, 2).reshape(row_count, ATT), maxima.T, totals.T)


def general(
    stream, latents, time_mod, block_mod, w_qkv, qk_gain, w_out, head_mod, w_head, noise_level
):
    slab_count = lax.axis_size("slab")
    seq_count = lax.axis_size("seq")
    slab_index = lax.axis_index("slab")
    seq_index = lax.axis_index("seq")
    group_rows = TOK_DEV * seq_count
    hidden = stream[0].astype(jnp.float32)
    modulation = block_mod + time_mod[0]
    modded = (layer_norm(hidden) * (1.0 + modulation[1]) + modulation[0]).astype(jnp.bfloat16)
    columns = jnp.dot(
        lax.all_gather(modded, "seq", axis=0, tiled=True), w_qkv, preferred_element_type=jnp.float32
    ).astype(jnp.bfloat16)
    own_position = (slab_index * group_rows + seq_index * TOK_DEV + jnp.arange(TOK_DEV)).astype(
        jnp.float32
    )
    full_mixed = lax.all_gather(columns, "seq", axis=1, tiled=True)
    own_mixed = lax.dynamic_slice_in_dim(full_mixed, seq_index * TOK_DEV, TOK_DEV, 0)
    own_queries = norm_rope(own_mixed[:, :ATT], qk_gain[0], own_position)
    group_position = (slab_index * group_rows + jnp.arange(group_rows)).astype(jnp.float32)
    group_keys = norm_rope(full_mixed[:, ATT : 2 * ATT], qk_gain[1], group_position)
    group_values = full_mixed[:, 2 * ATT :]
    all_queries = lax.all_gather(own_queries[None], "slab", axis=0, tiled=True)
    slab_ids = jnp.arange(slab_count)
    output, maxima, totals = group_parts(
        all_queries.reshape(slab_count * TOK_DEV, ATT), group_keys, group_values
    )
    usable = (slab_ids >= slab_index)[:, None, None]
    output = jnp.where(usable, output.reshape(slab_count, TOK_DEV, ATT), 0.0)
    maxima = jnp.where(usable, maxima.reshape(slab_count, TOK_DEV, HEADS), -1e30)
    totals = jnp.where(usable, totals.reshape(slab_count, TOK_DEV, HEADS), 0.0)
    recv_out, recv_max, recv_sum = (
        lax.all_to_all(output, "slab", split_axis=0, concat_axis=0, tiled=True),
        lax.all_to_all(maxima, "slab", split_axis=0, concat_axis=0, tiled=True),
        lax.all_to_all(totals, "slab", split_axis=0, concat_axis=0, tiled=True),
    )
    highest = jnp.max(recv_max, axis=0)
    weights = jnp.exp(recv_max - highest)
    total_sum = jnp.sum(recv_sum * weights, axis=0)
    accum = jnp.sum(
        recv_out.reshape(slab_count, TOK_DEV, HEADS, HEAD_DIM) * weights[..., None], axis=0
    )
    attended = (accum / total_sum[..., None]).reshape(TOK_DEV, ATT).astype(jnp.bfloat16)
    projected = jnp.dot(attended, w_out, preferred_element_type=jnp.float32)
    updated = hidden + modulation[2] * projected
    head_in = (layer_norm(updated) * (1.0 + head_mod[0, 1]) + head_mod[0, 0]).astype(jnp.bfloat16)
    velocity = jnp.dot(head_in, w_head, preferred_element_type=jnp.float32)
    table = sigma_table()
    level_ids = jnp.arange(LEVELS + 1)
    current_level = noise_level[0]
    sigma_now = jnp.sum(jnp.where(level_ids == current_level, table, 0.0))
    sigma_next = jnp.sum(jnp.where(level_ids == current_level - 1, table, 0.0))
    stepped = latents[0] + (sigma_next - sigma_now) * velocity
    moved = from_behind(stepped[None], "slab", -1)
    return (updated.astype(jnp.bfloat16)[None], moved)


def vmem_call(kernel, outs, name, flops, scratch=(), placed=0):
    whole = pl.BlockSpec(memory_space=pltpu.VMEM)
    stay = pl.BlockSpec(memory_space=pltpu.HBM)

    def call(*operands):
        return pl.pallas_call(
            kernel,
            out_shape=[jax.ShapeDtypeStruct(shape, dtype) for shape, dtype in outs],
            in_specs=[whole] * (len(operands) - placed) + [stay] * placed,
            out_specs=[whole] * len(outs),
            scratch_shapes=list(scratch),
            compiler_params=pltpu.CompilerParams(vmem_limit_bytes=VMEM_LIMIT),
            cost_estimate=pl.CostEstimate(flops=flops, bytes_accessed=1 << 20, transcendentals=0),
            name=name,
        )(*operands)

    return call


def here():
    slab, seq = lax.axis_index("slab"), lax.axis_index("seq")
    return seq // 2, seq % 2, slab % 2, slab // 2


def dot_rows(left, right):
    return lax.dot_general(left, right, (((1,), (1,)), ((), ())), preferred_element_type=F32)


def modulated(rows, shift_scale):
    return (layer_norm(rows[...].astype(F32)) * shift_scale[1:2] + shift_scale[0:1]).astype(BF16)


def prepare_kernel(x0, time_mod, block_mod, modded, shift_scale):
    shift_scale[0:1] = block_mod[0:1] + time_mod[0]
    shift_scale[1:2] = 1.0 + (block_mod[1:2] + time_mod[1])
    modded[...] = modulated(x0, shift_scale)


def part_product(modded, weights, part):
    depth = weights.shape[0]
    at = pl.multiple_of(part * depth, depth)
    return jnp.dot(modded[:, pl.ds(at, depth)], weights[...], preferred_element_type=F32)


def early_kernel(x1, modded_own, shift_scale, w_own, modded, own):
    modded[:TOK_DEV, :] = modulated(x1, shift_scale)
    modded[TOK_DEV:, :] = modded_own[...]
    own[...] = jnp.dot(modded[...], w_own[...], preferred_element_type=F32).astype(BF16)


def project_kernel(
    x2, x3, modded_early, own_early, shift_scale, w_own, w_mine, w_last, w_chip,
    w_core, w_core_last, w_core_chip, far_out, near_out, keep_out, sums_out, modded, mixed,
):
    for place, rows in enumerate((x2, x3)):
        modded[place * TOK_DEV : (place + 1) * TOK_DEV, :] = modulated(rows, shift_scale)
    late = 2 * TOK_DEV
    modded[late:, :] = modded_early[...]
    line, side, core, chip = here()
    width = w_own.shape[1]
    own = jnp.dot(modded[:late, :], w_own[...], preferred_element_type=F32).astype(BF16)
    own = jnp.concatenate([own, own_early[...]], axis=0)
    total = part_product(modded, w_mine, 2 * chip + core)
    total += part_product(modded, w_core, 2 * chip + 1 - core)
    total += part_product(modded, w_chip, 2 * (1 - chip) + core)
    total += part_product(modded, w_core_chip, 2 * (1 - chip) + 1 - core)
    total += part_product(modded, w_last, 4 + core)
    other = (total + part_product(modded, w_core_last, 5 - core)).astype(BF16)
    mine = pl.multiple_of(side * width, width)
    there = pl.multiple_of((1 - side) * width, width)
    for place, step in enumerate((2, 3, 1, 0)):
        at = pl.multiple_of(jnp.bitwise_xor(line, step) * TOK_DEV, 16)
        rows = slice(place * TOK_DEV, (place + 1) * TOK_DEV)
        mixed[pl.ds(at, TOK_DEV), pl.ds(mine, width)] = own[rows]
        mixed[pl.ds(at, TOK_DEV), pl.ds(there, width)] = other[rows]
    ones = jnp.ones((16, PAIR), BF16)
    row_id = lax.broadcasted_iota(jnp.int32, (16, ROWS), 0)
    picked = jnp.zeros((16, ROWS), F32)
    for unit in range(3):
        values = mixed[:, unit * PAIR : (unit + 1) * PAIR].astype(F32)
        squares = values * values
        high = squares.astype(BF16)
        low = (squares - high.astype(F32)).astype(BF16)
        total = dot_rows(ones, high) + dot_rows(ones, low)
        kind = (line * 3 + unit) // LINE
        picked += jnp.where(row_id // 3 == kind, total, 0.0)
    picked = jnp.where(row_id < 6, picked, 0.0)
    first = picked.astype(BF16).astype(F32)
    second = (picked - first).astype(BF16).astype(F32)
    third = picked - first - second
    part = row_id % 3
    packed = jnp.where(part == 0, first, jnp.where(part == 1, second, third)).astype(BF16)
    padded = jnp.concatenate([packed, jnp.zeros((16, PAIR - ROWS), BF16)], axis=1)
    sums_out[...] = padded
    near_out[:ROWS, :] = mixed[:, PAIR : 2 * PAIR]
    near_out[ROWS:, :] = padded
    odd = line % 2
    at = pl.multiple_of((1 - odd) * 2 * PAIR, PAIR)
    far_out[:ROWS, :] = mixed[:, pl.ds(at, PAIR)]
    far_out[ROWS:, :] = padded
    at = pl.multiple_of(odd * 2 * PAIR, PAIR)
    keep_out[...] = mixed[:, pl.ds(at, PAIR)]


def step_size(levels):
    level = jnp.broadcast_to(levels[...], (1, HEAD_DIM))

    def sigma(level):
        fraction = level.astype(F32) / LEVELS
        return 5.0 * fraction / (1.0 + 4.0 * fraction)

    return sigma(level - 1) - sigma(level)


def row_scale(pieces, kind):
    wanted = lax.broadcasted_iota(jnp.int32, (16, 1), 0) // 3 == kind
    total = jnp.zeros((1, PAIR), F32)
    for piece in pieces:
        total += jnp.sum(jnp.where(wanted, piece, 0.0), axis=0, keepdims=True)
    scale = lax.rsqrt(total * (1.0 / ATT) + 1e-06)
    return jnp.transpose(jnp.broadcast_to(scale, (HEAD_DIM, PAIR)))[:ROWS]


def turn(values, scale, gains, kind, head, cos, sin):
    columns = slice(head * HEAD_DIM, (head + 1) * HEAD_DIM)
    at = pl.multiple_of(here()[0] * PAIR + head * HEAD_DIM, HEAD_DIM)
    scaled = values[:, columns] * scale * gains[kind : kind + 1, pl.ds(at, HEAD_DIM)]
    return (scaled * cos + pltpu.roll(scaled, HEAD_DIM // 2, axis=1) * sin).astype(BF16)


def keys_kernel(
    near, far, middle_sums, keep, own_sums, gains, cosines, sines, levels,
    kv_out, q_out, sums_out, size, units,
):
    line, _, _, _ = here()
    upper, odd = line // 2, line % 2
    slots = (
        jnp.where(upper == 1, 2, odd),
        jnp.where((line == 0) | (line == 3), 1, 0),
        jnp.where(upper == 0, 2, 1 - odd),
    )
    units[0] = keep[...]
    units[1] = near[:ROWS, :]
    units[2] = far[:ROWS, :]
    inner = (line == 1) | (line == 2)
    pieces = [
        own_sums[...].astype(F32), near[ROWS:, :].astype(F32), far[ROWS:, :].astype(F32),
        jnp.where(inner, middle_sums[...].astype(F32), 0.0),
    ]
    scale = row_scale(pieces, 1)
    values = units[slots[1]].astype(F32)
    for head in range(2):
        columns = slice(head * HEAD_DIM, (head + 1) * HEAD_DIM)
        kv_out[:, columns] = turn(values, scale, gains, 1, head, cosines[...], sines[...])
    kv_out[:, PAIR:] = units[slots[2]]
    size[...] = step_size(levels)
    q_out[...] = units[slots[0]]
    sums_out[...] = pieces[0] + pieces[1] + pieces[2] + pieces[3]


def queries_kernel(raw, sums, last_sums, gains, cosines, sines, q_out):
    line = here()[0]
    last = jnp.where(line == 3, last_sums[...].astype(F32), 0.0)
    scale = row_scale([sums[...], last], 0)
    values = raw[...].astype(F32)
    for head in range(2):
        columns = slice(head * HEAD_DIM, (head + 1) * HEAD_DIM)
        q_out[:, columns] = turn(values, scale, gains, 0, head, cosines[...], sines[...])


def attend_group(queries, one, two, head, counts=None):
    columns = slice(head * HEAD_DIM, (head + 1) * HEAD_DIM)
    value_columns = slice(PAIR + head * HEAD_DIM, PAIR + (head + 1) * HEAD_DIM)
    keys = jnp.concatenate([one[:, columns], two[:, columns]], axis=0)
    values = jnp.concatenate([one[:, value_columns], two[:, value_columns]], axis=0)
    ones = jnp.ones((2 * ROWS, HEAD_DIM), BF16)
    scores = dot_rows(queries[:, columns], keys) * HEAD_DIM ** (-0.5)
    maxima = jnp.max(scores, axis=-1, keepdims=True)
    weights = jnp.exp(scores - maxima).astype(BF16)
    output = jnp.dot(weights, jnp.concatenate([values, ones], axis=1), preferred_element_type=F32)
    if counts is not None:
        maxima = jnp.where(counts, maxima, -1e30)
    return output, maxima


def merged(parts):
    highest = functools.reduce(jnp.maximum, [maxima for _, maxima in parts])
    total = sum(output * jnp.exp(maxima - highest) for output, maxima in parts)
    return total, highest


def first_attend_kernel(queries, c0, c1, a0, a1, total_out, highest_out):
    chip = here()[3]
    for head in range(2):
        own = attend_group(queries, a0, a1, head)
        far = attend_group(queries, c0, c1, head, chip == 1)
        total, highest = merged([own, far])
        total_out[head] = total
        highest_out[head] = jnp.broadcast_to(highest, (ROWS, HEAD_DIM))


def last_attend_kernel(
    queries, b0, b1, d0, d1, total_in, highest_in, o3, o2, o1, o0, result
):
    line, _, core, chip = here()
    for head in range(2):
        near = attend_group(queries, b0, b1, head, core == 1)
        far = attend_group(queries, d0, d1, head, chip == 1)
        total, _ = merged([(total_in[head], highest_in[head, :, :1]), near, far])
        columns = slice(head * HEAD_DIM, (head + 1) * HEAD_DIM)
        result[:, columns] = (total[:, :HEAD_DIM] / total[:, HEAD_DIM:]).astype(BF16)
    for step, out in enumerate((o0, o1, o2, o3)):
        at = pl.multiple_of(jnp.bitwise_xor(line, step) * TOK_DEV, 16)
        out[...] = result[pl.ds(at, TOK_DEV), :]


def load(sources, held, arrived):
    copies = [
        pltpu.make_async_copy(source, target, arrived.at[i])
        for i, (source, target) in enumerate(zip(sources, held))
    ]
    for copy in copies:
        copy.start()
    return copies


def times_w_out(rows, w_out, step):
    at = pl.multiple_of(jnp.bitwise_xor(here()[0], step) * PAIR, PAIR)
    return jnp.dot(rows[...], w_out[pl.ds(at, PAIR), :], preferred_element_type=F32)


def begin_kernel(
    r0, w_out, stream_in, time_in, block_in, head_in, base, vectors,
    stream, time_mod, block_mod, head_mod, arrived,
):
    copies = load(
        (stream_in, time_in, block_in, head_in), (stream, time_mod, block_mod, head_mod), arrived
    )
    projected = times_w_out(r0, w_out, 0)
    for copy in copies:
        copy.wait()
    gate = block_mod[2:3] + time_mod[2]
    base[...] = stream[...].astype(F32) + gate * projected
    vectors[0:1] = gate
    vectors[1:2] = 1.0 + head_mod[1:2]
    vectors[2:3] = head_mod[0:1]


def finish_kernel(
    r2, r3, r1, w_out, base, vectors, w_head, size, latents_in, stream_out, latents_out,
    latents, arrived,
):
    copies = load((latents_in,), (latents,), arrived)
    projected = times_w_out(r3, w_out, 3) + times_w_out(r2, w_out, 2) + times_w_out(r1, w_out, 1)
    updated = base[...] + vectors[0:1] * projected
    stream_out[...] = updated
    head_in = (layer_norm(updated) * vectors[1:2] + vectors[2:3]).astype(BF16)
    velocity = dot_rows(head_in, w_head[...])

    copies[0].wait()
    latents_out[...] = latents[...] + size[0:1, :CHAN] * velocity


def lines(
    stream, latents, time_mod, block_mod, w_qkv, qk_gain, w_out, head_mod, w_head, noise_level
):
    slab, seq = lax.axis_index("slab"), lax.axis_index("seq")
    side, core = seq % 2, slab % 2

    def along(step, value):
        return lax.ppermute(value, "seq", [(i, i ^ (2 * step)) for i in range(2 * LINE)])

    def middle(value):
        pairs = [(i, i ^ 6 if i in (2, 3, 4, 5) else i ^ 1) for i in range(2 * LINE)]
        return lax.ppermute(value, "seq", pairs)

    def across(value):
        return lax.ppermute(value, "seq", [(i, i ^ 1) for i in range(2 * LINE)])

    def cores(value):
        return lax.ppermute(value, "slab", [(i, i ^ 1) for i in range(4)])

    def chips(value):
        return lax.ppermute(value, "slab", [(i, i ^ 2) for i in range(4)])

    def chips_and_sides(value):
        count = 2 * LINE
        pairs = [
            (s * count + i, (s ^ 2) * count + (i ^ 1 if s < 2 else i))
            for s in range(4)
            for i in range(count)
        ]
        return lax.ppermute(value, ("slab", "seq"), pairs)

    rows = stream[0]
    time_rows = time_mod.transpose(1, 0, 2)
    depth = D // 6
    half_mine = lax.dynamic_slice_in_dim(w_qkv, slab * depth, depth, 0)
    half_last = lax.dynamic_slice_in_dim(w_qkv, (4 + core) * depth, depth, 0)
    w_mine, w_last = across(half_mine), across(half_last)
    late_rows, _ = lax.optimization_barrier((rows, half_mine))
    x1, x2, x3 = along(1, rows), along(2, rows), along(3, rows)

    at = (jnp.arange(LINE)[:, None] * 2 + side) * TOK_DEV + jnp.arange(TOK_DEV)[None]
    position = (slab * (2 * LINE * TOK_DEV) + at.reshape(ROWS)).astype(F32)
    halves = HEAD_DIM // 2
    frequency = jnp.power(10000.0, -jnp.arange(halves).astype(F32) / halves)
    angles = position[:, None] * frequency[None]
    cosines, sines = jnp.cos(angles), jnp.sin(angles)
    cosines = jnp.concatenate([cosines, cosines], axis=1)
    sines = jnp.concatenate([-sines, sines], axis=1)
    modded_own, shift_scale = vmem_call(
        prepare_kernel, [((TOK_DEV, D), BF16), ((2, D), F32)], "prepare", 1 << 20
    )(rows, time_rows, block_mod)
    w_chip = chips(w_mine)
    w_last, modded_own, shift_scale = lax.optimization_barrier((w_last, modded_own, shift_scale))
    w_core_last = cores(w_last)
    w_mine, w_chip = lax.optimization_barrier((w_mine, w_chip))
    w_core, w_core_chip = cores(w_mine), cores(w_chip)
    modded_early, own_early = vmem_call(
        early_kernel,
        [((2 * TOK_DEV, D), BF16), ((2 * TOK_DEV, w_qkv.shape[1]), BF16)], "early", 1 << 26,
    )(x1, modded_own, shift_scale, w_qkv)
    message = (ROWS + 16, PAIR)
    far, near, keep, sums = vmem_call(
        project_kernel,
        [(message, BF16), (message, BF16), ((ROWS, PAIR), BF16), ((16, PAIR), BF16)],
        "project", 1 << 28, [pltpu.VMEM((ROWS, D), BF16), pltpu.VMEM((ROWS, 3 * PAIR), BF16)],
    )(
        x2, x3, modded_early, own_early, shift_scale, w_qkv,
        w_mine, w_last, w_chip, w_core, w_core_last, w_core_chip,
    )
    near, middle_sums, far = along(1, near), middle(sums), along(2, far)
    pairs, raw_queries, some_sums, size = vmem_call(
        keys_kernel,
        [((ROWS, 2 * PAIR), BF16), ((ROWS, PAIR), BF16), ((16, PAIR), F32), ((1, HEAD_DIM), F32)],
        "rope_keys", 1 << 22, [pltpu.VMEM((3, ROWS, PAIR), BF16)],
    )(near, far, middle_sums, keep, sums, qk_gain, cosines, sines, noise_level[None])
    _, late_sums = lax.optimization_barrier((some_sums, sums))
    chip_pairs, side_pairs, last_sums = chips(pairs), across(pairs), along(3, late_sums)
    both_pairs = chips_and_sides(pairs)
    chip_pairs, side_pairs = lax.optimization_barrier((chip_pairs, side_pairs))
    both_pairs, last_sums = lax.optimization_barrier((both_pairs, last_sums))
    (queries,) = vmem_call(queries_kernel, [((ROWS, PAIR), BF16)], "rope_queries", 1 << 22)(
        raw_queries, some_sums, last_sums, qk_gain, cosines, sines
    )
    state = [((2, ROWS, PAIR), F32), ((2, ROWS, HEAD_DIM), F32)]
    now = vmem_call(first_attend_kernel, state, "attend_first", 1 << 27)(
        queries, chip_pairs, both_pairs, pairs, side_pairs
    )
    core_pairs = cores(pairs)
    core_side, core_chip, core_both = cores(side_pairs), cores(chip_pairs), cores(both_pairs)
    part3, part2, part1, part0 = vmem_call(
        last_attend_kernel, [((TOK_DEV, PAIR), BF16)] * 4, "attend_last", 1 << 27,
        [pltpu.VMEM((ROWS, PAIR), BF16)],
    )(queries, core_pairs, core_side, core_chip, core_both, *now)
    late = [along(2, part2), along(3, part3), along(1, part1)]
    loaded = (rows, time_rows, block_mod, head_mod[0])
    base, vectors = vmem_call(
        begin_kernel, [((TOK_DEV, D), F32), ((8, D), F32)], "begin", 1 << 28,
        [pltpu.VMEM(v.shape, v.dtype) for v in loaded] + [pltpu.SemaphoreType.DMA((len(loaded),))],
        placed=len(loaded),
    )(part0, w_out, *loaded)
    updated, stepped = vmem_call(
        finish_kernel, [((TOK_DEV, D), F32), ((TOK_DEV, CHAN), F32)], "finish", 1 << 28,
        [pltpu.VMEM((TOK_DEV, CHAN), F32), pltpu.SemaphoreType.DMA((1,))], placed=1,
    )(*late, w_out, base, vectors, w_head.T, size, latents[0])
    return (updated.astype(BF16)[None], from_behind(stepped[None], "slab", -1))


def solution(mesh):
    in_specs = (
        P("slab", "seq", None),
        P("slab", "seq", None),
        P("slab", None, None),
        P(),
        P(None, "seq"),
        P(),
        P(),
        P("slab", None, None),
        P(),
        P("slab"),
    )
    out_specs = (P("slab", "seq", None), P("slab", "seq", None))
    local = lines if tuple(mesh.shape.values()) == (4, 2 * LINE) else general
    return jax.shard_map(local, mesh=mesh, in_specs=in_specs, out_specs=out_specs, check_vma=False)
```
